128 devices in a mesh: gx: 16 (over z, x), gy: 8 (over y, core).
Axes of the slice: x: 4, y: 4, z: 4, core: 2. Of those that a mesh axis runs over, the one named last changes fastest.
Arguments:
- level_set: float32 [512, 256, 128], P('gx', 'gy'), may hold values from -6 to 6
- sensitivity: float32 [512, 256, 128], P('gx', 'gy'), may hold values from -6 to 6
- smooth_taps: float32 [25], replicated, may hold values from 0.1 to 0.3
- slope_taps: float32 [25], replicated, as said below
- band: int32 [32, 16, 4], P('gx', 'gy'), may hold values from 0 to 1
- time_step: float32 [1], replicated, may hold values from 0.05 to 0.15
Outputs:
- updated: float32 [512, 256, 128], P('gx', 'gy')
The draws below stay inside these ranges and needn't reach their ends.
Inputs may be any that keep to these rules, and one draw needn't show every extreme that they name: slope_taps[24 - k] = -slope_taps[k]; the middle tap is zero.
All inputs are finite; a program needn't handle non-finite values.
Results may differ from the reference program's by a relative error of at most 0.00002.
Values sent between devices are 32-bit elements; how exact they have to be, the bound alone decides.
No kernel may reach another device: no remote copies, remote signals or barrier semaphores. Data moves between devices by JAX's collectives and lax.ppermute only.
A program may use at most 64 MiB of HBM per device.

```python
import math
import jax
import jax.numpy as jnp
from jax import lax

NZ = 128
TAPS = 25
BX = 16
BY = 16
BZ = 32
UPDATES = 2
NX = 512
NY = 256


def draw_slope_taps(key, part):
    halves = jax.random.normal(key, (TAPS // 2,), jnp.float32) * 0.3
    return jnp.concatenate([-halves[::-1], jnp.zeros((1,), jnp.float32), halves])


def draw_band(key, part):
    shape = (NX // BX, NY // BY, NZ // BZ)
    rolls = jax.random.randint(key, shape, 0, 8)
    levels = jax.random.randint(jax.random.fold_in(key, 1), (shape[0], 1, 1), 2, 9)
    return (rolls < levels).astype(jnp.int32)


def shard_levels(rng, extent, cuts, low, top_value):
    def one(axis_at, blocks):
        draws = jax.random.uniform(jax.random.fold_in(jax.random.fold_in(rng, 6), axis_at), (blocks,), jnp.float32, low / len(cuts), top_value / len(cuts))
        return jnp.repeat(jnp.exp(draws), extent[axis_at] // blocks).reshape((-1,) + (1,) * (len(extent) - axis_at - 1))

    loudness = one(*cuts[0])
    for cut in cuts[1:]:
        loudness = loudness * one(*cut)
    return loudness


def bell_draw(own_key, shape, width, bound, split=(), held_as=jnp.bfloat16):
    values = jax.random.normal(own_key, shape, jnp.float32) * width
    if len(split) > 0:
        values = shard_levels(own_key, shape, split, -0.22, 0.18) * values
    return jnp.clip(values, min=-bound, max=bound).astype(held_as)


def setup_inputs(seed: int = 0) -> dict:
    seeds = jax.random.split(jax.random.key(seed), 7)
    level_set = bell_draw(seeds[0], (NX, NY, NZ), 1.0, 6.0, ((0, 16), (1, 8)), jnp.float32)
    sensitivity = bell_draw(seeds[1], (NX, NY, NZ), 1.0, 6.0, ((0, 16), (1, 8)), jnp.float32)
    smooth_taps = jnp.clip(jnp.exp(jax.random.uniform(seeds[2], (TAPS,), jnp.float32, math.log(0.1), math.log(0.3))), 0.1, 0.3)
    slope_taps = draw_slope_taps(jax.random.fold_in(seeds[6], 71), 0)
    band = draw_band(jax.random.fold_in(seeds[6], 71), 0)
    time_step = jnp.clip(jax.random.uniform(seeds[5], (1,), jnp.float32, 0.05, 0.15), 0.05, 0.15)
    return {"level_set": level_set, "sensitivity": sensitivity, "smooth_taps": smooth_taps, "slope_taps": slope_taps, "band": band, "time_step": time_step}


def filt(field, taps, axis):
    length = field.shape[axis]
    widths = [(0, 0)] * field.ndim
    widths[axis] = (12, 12)
    padded = jnp.pad(field, widths)
    summed = taps[0] * lax.slice_in_dim(padded, 0, length, axis=axis)
    for offset in range(1, 25):
        summed = summed + taps[offset] * lax.slice_in_dim(padded, offset, offset + length, axis=axis)
    return summed

def reference(level_set, sensitivity, smooth_taps, slope_taps, band, time_step):
    velocity = filt(filt(filt(sensitivity, smooth_taps, 2), smooth_taps, 0), smooth_taps, 1)
    padded_v = jnp.pad(velocity, 1)
    speed = (padded_v[1:-1, 1:-1, 1:-1] + padded_v[2:, 1:-1, 1:-1] + padded_v[:-2, 1:-1, 1:-1] + padded_v[1:-1, 2:, 1:-1] + padded_v[1:-1, :-2, 1:-1] + padded_v[1:-1, 1:-1, 2:] + padded_v[1:-1, 1:-1, :-2]) / 7.0
    blocks_x, blocks_y, blocks_z = band.shape
    mask = jnp.broadcast_to(band.astype(jnp.float32)[:, None, :, None, :, None], (blocks_x, BX, blocks_y, BY, blocks_z, BZ)).reshape(level_set.shape)
    step_size = time_step[0]
    phi = level_set
    for update_index in range(UPDATES):
        depth_smooth = filt(phi, smooth_taps, 2)
        depth_slope = filt(phi, slope_taps, 2)
        cross_smooth = filt(depth_smooth, smooth_taps, 0)
        cross_slope = filt(depth_smooth, slope_taps, 0)
        third_smooth = filt(depth_slope, smooth_taps, 0)
        grad_x = filt(cross_slope, smooth_taps, 1)
        grad_y = filt(cross_smooth, slope_taps, 1)
        grad_z = filt(third_smooth, smooth_taps, 1)
        magnitude = jnp.sqrt(grad_x * grad_x + grad_y * grad_y + grad_z * grad_z + 1.0)
        normal_x = jnp.pad(grad_x / magnitude, ((1, 1), (0, 0), (0, 0)))
        normal_y = jnp.pad(grad_y / magnitude, ((0, 0), (1, 1), (0, 0)))
        normal_z = jnp.pad(grad_z / magnitude, ((0, 0), (0, 0), (1, 1)))
        curvature = 0.5 * (normal_x[2:] - normal_x[:-2]) + 0.5 * (normal_y[:, 2:] - normal_y[:, :-2]) + 0.5 * (normal_z[:, :, 2:] - normal_z[:, :, :-2])
        phi = phi - mask * step_size * magnitude * (speed - 0.5 * curvature)
    return phi
```

```python
import functools

import jax
import jax.numpy as jnp
from jax import lax
from jax.experimental import pallas as pl
from jax.experimental.pallas import tpu as pltpu
from jax.sharding import PartitionSpec as P

UPDATES = 2
REACH = 13
SLAB = 16
SIDE = 32
RIM = 40
WIDE = 64
DEPTH = 128
TAPS = 25
SPAN = SIDE + 2 * REACH

IN_COORDS = list(range(SIDE + REACH)) + list(range(WIDE - REACH, WIDE))
OUT_ROWS = [RIM - 1] + list(range(SIDE + 1))


def split_rows(value):
    high = value.astype(jnp.bfloat16)
    low = (value - high.astype(jnp.float32)).astype(jnp.bfloat16)
    return high, low


def tap_select(index, taps):
    total = jnp.zeros(index.shape, jnp.float32)
    for k in range(TAPS):
        total = jnp.where(index == k, taps[k], total)
    return total


def side_matrix(low_open, high_open, smooth, slope):
    shape = (RIM, 3 * WIDE)
    row = lax.broadcasted_iota(jnp.int32, shape, 0)
    column = lax.broadcasted_iota(jnp.int32, shape, 1)
    place = column & (WIDE - 1)
    source = jnp.where(place < WIDE - SLAB, place, place - WIDE)
    target = jnp.where(row < RIM - 1, row, -1)
    index = source - target + TAPS // 2
    inside = (row < SIDE) | ((row == SIDE) & (high_open != 0)) | ((row == RIM - 1) & (low_open != 0))
    index = jnp.where(inside, index, -1)
    parts = []
    for taps in (smooth, slope):
        full = tap_select(index, taps)
        high = full.astype(jnp.bfloat16).astype(jnp.float32)
        parts.append(jnp.where(column < 2 * WIDE, high, full - high))
    return jnp.concatenate(parts, axis=0).astype(jnp.bfloat16)


def prepare_kernel(smooth, slope, band, step, edges, along_x, along_y, depth_s, depth_g, gain):
    along_x[...] = side_matrix(edges[0], edges[1], smooth, slope)
    along_y[...] = side_matrix(edges[2], edges[3], smooth, slope)
    shape = (DEPTH, DEPTH)
    index = (
        lax.broadcasted_iota(jnp.int32, shape, 0)
        - lax.broadcasted_iota(jnp.int32, shape, 1)
        + TAPS // 2
    )
    for taps, out in ((smooth, depth_s), (slope, depth_g)):
        high, low = split_rows(tap_select(index, taps))
        out[0:DEPTH, :] = high
        out[DEPTH : 2 * DEPTH, :] = high
        out[2 * DEPTH :, :] = low
    blocks_x, blocks_y, blocks_z = 2, 2, 4
    lane = lax.broadcasted_iota(jnp.int32, (SIDE // blocks_y, DEPTH), 1) // (DEPTH // blocks_z)
    for p in range(blocks_x):
        for q in range(blocks_y):
            value = jnp.zeros(lane.shape, jnp.float32)
            for r in range(blocks_z):
                entry = band[p, q, r].astype(jnp.float32) * step[0]
                value = jnp.where(lane == r, entry, value)
            gain[p, q * (SIDE // blocks_y) : (q + 1) * (SIDE // blocks_y), :] = value


def prepare(smooth, slope, band, step, edges):
    smem = pl.BlockSpec(memory_space=pltpu.SMEM)
    vmem = pl.BlockSpec(memory_space=pltpu.VMEM)
    return pl.pallas_call(
        prepare_kernel,
        out_shape=(
            jax.ShapeDtypeStruct((2 * RIM, 3 * WIDE), jnp.bfloat16),
            jax.ShapeDtypeStruct((2 * RIM, 3 * WIDE), jnp.bfloat16),
            jax.ShapeDtypeStruct((3 * DEPTH, DEPTH), jnp.bfloat16),
            jax.ShapeDtypeStruct((3 * DEPTH, DEPTH), jnp.bfloat16),
            jax.ShapeDtypeStruct((2, SIDE, DEPTH), jnp.float32),
        ),
        in_specs=[smem] * 5,
        out_specs=(vmem,) * 5,
    )(smooth, slope, band, step, edges)


def fill_extended(extended, own, x_next, x_prev, y_next, y_prev):
    low = WIDE - REACH
    high = SIDE + REACH
    extended[0:SIDE, 0:SIDE, :] = own
    extended[SIDE:high, 0:SIDE, :] = x_next
    extended[high:low, :, :] = jnp.zeros((low - high, WIDE, DEPTH), jnp.float32)
    extended[low:WIDE, 0:SIDE, :] = x_prev
    for start, slab in ((SIDE, y_next), (WIDE - SLAB, y_prev)):
        extended[0:high, start : start + SLAB, :] = slab[0:high]
        extended[low:WIDE, start : start + SLAB, :] = slab[high:SPAN]


def stacked_parts(value):
    high, low = split_rows(value)
    return jnp.concatenate([high, low, high], axis=0)


def lane_parts(value):
    high, low = split_rows(value)
    return jnp.concatenate([high, low, high], axis=1)


def take_place(block, place):
    outer, inner, depth = block.shape
    return block.reshape(outer * inner, depth)[pl.ds(place, outer, stride=inner), :]


def along_x_stage(extended, crossed, matrix):
    rows = matrix.shape[0]
    crossed[SIDE + REACH : WIDE - REACH, :, :] = jnp.zeros(
        (WIDE - 2 * REACH - SIDE, rows, DEPTH), jnp.float32
    )
    for pair in range(0, len(IN_COORDS), 2):
        places = IN_COORDS[pair : pair + 2]
        value = jnp.concatenate([take_place(extended, y) for y in places], axis=1)
        out = jnp.dot(matrix, stacked_parts(value), preferred_element_type=jnp.float32)
        for at, y in enumerate(places):
            crossed[y, :, :] = out[:, at * DEPTH : (at + 1) * DEPTH]


def gradient_kernel(
    own, x_next, x_prev, y_next, y_prev, along_x, along_y, depth_s, depth_g, speed, gain, out,
    extended, crossed, flat_s, flat_g, normals, lengths,
):
    fill_extended(extended, own[...], x_next[...], x_prev[...], y_next[...], y_prev[...])
    along_x_stage(extended, crossed, along_x[...])
    matrix = along_y[...]
    for at, row in enumerate(OUT_ROWS):
        value = jnp.concatenate(
            [take_place(crossed, row + kind * RIM) for kind in range(2)], axis=1
        )
        got = jnp.dot(matrix, stacked_parts(value), preferred_element_type=jnp.float32)
        flat_s[at, 0:RIM, :] = got[0:RIM, DEPTH:]
        flat_s[at, RIM:, :] = got[RIM:, :DEPTH]
        flat_g[at, :, :] = got[0:RIM, :DEPTH]
    weights_s = depth_s[...]
    weights_g = depth_g[...]
    for at in range(0, SIDE + 2, 2):
        cross = jnp.dot(
            lane_parts(flat_s[at : at + 2].reshape(4 * RIM, DEPTH)), weights_s,
            preferred_element_type=jnp.float32,
        )
        deep = jnp.dot(
            lane_parts(flat_g[at : at + 2].reshape(2 * RIM, DEPTH)), weights_g,
            preferred_element_type=jnp.float32,
        )
        for half in range(2):
            grad_x = cross[2 * half * RIM : (2 * half + 1) * RIM]
            grad_y = cross[(2 * half + 1) * RIM : (2 * half + 2) * RIM]
            grad_z = deep[half * RIM : (half + 1) * RIM]
            square = grad_x * grad_x + grad_y * grad_y + grad_z * grad_z + 1.0
            inverse = lax.rsqrt(square)
            normals[0, at + half, :, :] = grad_x * inverse
            normals[1, at + half, :, :] = grad_y * inverse
            normals[2, at + half, :, :] = grad_z * inverse
            lengths[at + half, :, :] = square * inverse
    lane = lax.broadcasted_iota(jnp.int32, (SIDE, DEPTH), 1)
    for x in range(SIDE):
        at = x + 1
        across = normals[1, at, :, :]
        deep = normals[2, at, 0:SIDE, :]
        bend = normals[0, at + 1, 0:SIDE, :] - normals[0, at - 1, 0:SIDE, :]
        bend += (pltpu.roll(across, RIM - 1, 0) - pltpu.roll(across, 1, 0))[0:SIDE]
        bend += jnp.where(lane < DEPTH - 1, pltpu.roll(deep, DEPTH - 1, 1), 0.0)
        bend -= jnp.where(lane > 0, pltpu.roll(deep, 1, 1), 0.0)
        push = gain[x // (SIDE // 2)] * lengths[at, 0:SIDE, :]
        out[x, :, :] = own[x, :, :] - push * (speed[x, :, :] - 0.25 * bend)


def speed_kernel(
    own, x_next, x_prev, y_next, y_prev, along_x, along_y, depth_s, out,
    extended, crossed, flat_s, velocity,
):
    fill_extended(extended, own[...], x_next[...], x_prev[...], y_next[...], y_prev[...])
    along_x_stage(extended, crossed, along_x[0:RIM + 8, :])
    matrix = along_y[0:RIM + 8, :]
    for pair in range(0, len(OUT_ROWS), 2):
        value = jnp.concatenate(
            [take_place(crossed, row) for row in OUT_ROWS[pair : pair + 2]], axis=1
        )
        got = jnp.dot(matrix, stacked_parts(value), preferred_element_type=jnp.float32)
        for half in range(2):
            flat_s[pair + half, :, :] = got[0:RIM, half * DEPTH : (half + 1) * DEPTH]
    weights = depth_s[...]
    for at in range(0, SIDE + 2, 2):
        got = jnp.dot(
            lane_parts(flat_s[at : at + 2].reshape(2 * RIM, DEPTH)), weights,
            preferred_element_type=jnp.float32,
        )
        velocity[at : at + 2, :, :] = got.reshape(2, RIM, DEPTH)
    lane = lax.broadcasted_iota(jnp.int32, (SIDE, DEPTH), 1)
    for x in range(SIDE):
        at = x + 1
        rim = velocity[at, :, :]
        centre = rim[0:SIDE]
        total = centre + velocity[at + 1, 0:SIDE, :] + velocity[at - 1, 0:SIDE, :]
        total += (pltpu.roll(rim, RIM - 1, 0) + pltpu.roll(rim, 1, 0))[0:SIDE]
        total += jnp.where(lane < DEPTH - 1, pltpu.roll(centre, DEPTH - 1, 1), 0.0)
        total += jnp.where(lane > 0, pltpu.roll(centre, 1, 1), 0.0)
        out[x, :, :] = total / 7.0


def neighbours(forward_block, backward_block, axis):
    count = lax.axis_size(axis)
    forward = [(i, i + 1) for i in range(count - 1)]
    backward = [(target, source) for source, target in forward]
    return lax.ppermute(backward_block, axis, backward), lax.ppermute(forward_block, axis, forward)


def gather_halos(block):
    x_next, x_prev = neighbours(block[..., SIDE - REACH :, :, :], block[..., :REACH, :, :], "gx")

    def slab(low, high):
        return jnp.concatenate(
            [part[..., low:high, :] for part in (block, x_next, x_prev)], axis=-3
        )

    y_next, y_prev = neighbours(slab(SIDE - SLAB, SIDE), slab(0, SLAB), "gy")
    return block, x_next, x_prev, y_next, y_prev


def call_kernel(body, fields, others, field, scratch):
    def whole(array):
        return pl.BlockSpec(array.shape, lambda i, rank=array.ndim: (0,) * rank)

    def one(array):
        if array.ndim == 3:
            return whole(array)
        return pl.BlockSpec((None,) + array.shape[1:], lambda i: (field, 0, 0, 0))

    return pl.pallas_call(
        body,
        grid=(1,),
        out_shape=jax.ShapeDtypeStruct((SIDE, SIDE, DEPTH), jnp.float32),
        in_specs=[one(f) for f in fields] + [whole(o) for o in others],
        out_specs=pl.BlockSpec((SIDE, SIDE, DEPTH), lambda i: (0, 0, 0)),
        scratch_shapes=[pltpu.VMEM(shape, jnp.float32) for shape in scratch],
        compiler_params=pltpu.CompilerParams(vmem_limit_bytes=48 * 1024 * 1024),
    )(*fields, *others)


def per_device(level_set, sensitivity, smooth_taps, slope_taps, band, time_step):
    edges = []
    for axis in ("gx", "gy"):
        at = lax.axis_index(axis)
        edges += [at > 0, at < lax.axis_size(axis) - 1]
    edges = jnp.stack(edges).astype(jnp.int32)
    along_x, along_y, depth_s, depth_g, gain = prepare(
        smooth_taps, slope_taps, band, time_step, edges
    )
    fields = gather_halos(jnp.stack([sensitivity, level_set]))
    rim = SIDE + 2
    speed = call_kernel(
        speed_kernel, fields, (along_x, along_y, depth_s), 0,
        [(WIDE, WIDE, DEPTH), (WIDE, RIM + 8, DEPTH), (rim, RIM, DEPTH), (rim, RIM, DEPTH)],
    )
    phi = level_set
    for update in range(UPDATES):
        if update > 0:
            fields = gather_halos(phi)
        phi = call_kernel(
            gradient_kernel, fields, (along_x, along_y, depth_s, depth_g, speed, gain), 1,
            [
                (WIDE, WIDE, DEPTH), (WIDE, 2 * RIM, DEPTH), (rim, 2 * RIM, DEPTH),
                (rim, RIM, DEPTH), (3, rim, RIM, DEPTH), (rim, RIM, DEPTH),
            ],
        )
    return phi


def solution(mesh):
    return jax.shard_map(
        per_device,
        mesh=mesh,
        in_specs=(P("gx", "gy", None), P("gx", "gy", None), P(), P(), P("gx", "gy", None), P()),
        out_specs=P("gx", "gy", None),
        check_vma=False,
    )
```

```python
import functools

import jax
import jax.numpy as jnp
from jax import lax
from jax.experimental import pallas as pl
from jax.experimental.pallas import tpu as pltpu
from jax.sharding import PartitionSpec as P

UPDATES = 2
REACH = 13
SLAB = 16
SIDE = 32
RIM = 40
WIDE = 64
DEPTH = 128
TAPS = 25
SPAN = SIDE + 2 * REACH

IN_COORDS = list(range(SIDE + REACH)) + list(range(WIDE - REACH, WIDE))
OUT_ROWS = [RIM - 1] + list(range(SIDE + 1))


def split_rows(value):
    high = value.astype(jnp.bfloat16)
    low = (value - high.astype(jnp.float32)).astype(jnp.bfloat16)
    return high, low


def tap_select(index, taps):
    total = jnp.zeros(index.shape, jnp.float32)
    for k in range(TAPS):
        total = jnp.where(index == k, taps[k], total)
    return total


def side_matrix(low_open, high_open, smooth, slope):
    shape = (RIM, 3 * WIDE)
    row = lax.broadcasted_iota(jnp.int32, shape, 0)
    column = lax.broadcasted_iota(jnp.int32, shape, 1)
    place = column & (WIDE - 1)
    source = jnp.where(place < WIDE - SLAB, place, place - WIDE)
    target = jnp.where(row < RIM - 1, row, -1)
    index = source - target + TAPS // 2
    inside = (row < SIDE) | ((row == SIDE) & (high_open != 0)) | ((row == RIM - 1) & (low_open != 0))
    index = jnp.where(inside, index, -1)
    parts = []
    for taps in (smooth, slope):
        full = tap_select(index, taps)
        high = full.astype(jnp.bfloat16).astype(jnp.float32)
        parts.append(jnp.where(column < 2 * WIDE, high, full - high))
    return jnp.concatenate(parts, axis=0).astype(jnp.bfloat16)


def prepare_kernel(smooth, slope, band, step, edges, along_x, along_y, depth_s, depth_g, gain):
    along_x[...] = side_matrix(edges[0], edges[1], smooth, slope)
    along_y[...] = side_matrix(edges[2], edges[3], smooth, slope)
    shape = (DEPTH, DEPTH)
    index = (
        lax.broadcasted_iota(jnp.int32, shape, 0)
        - lax.broadcasted_iota(jnp.int32, shape, 1)
        + TAPS // 2
    )
    for taps, out in ((smooth, depth_s), (slope, depth_g)):
        high, low = split_rows(tap_select(index, taps))
        out[0:DEPTH, :] = high
        out[DEPTH : 2 * DEPTH, :] = high
        out[2 * DEPTH :, :] = low
    blocks_x, blocks_y, blocks_z = 2, 2, 4
    lane = lax.broadcasted_iota(jnp.int32, (SIDE // blocks_y, DEPTH), 1) // (DEPTH // blocks_z)
    for p in range(blocks_x):
        for q in range(blocks_y):
            value = jnp.zeros(lane.shape, jnp.float32)
            for r in range(blocks_z):
                entry = band[p, q, r].astype(jnp.float32) * step[0]
                value = jnp.where(lane == r, entry, value)
            gain[p, q * (SIDE // blocks_y) : (q + 1) * (SIDE // blocks_y), :] = value


def prepare(smooth, slope, band, step, edges):
    smem = pl.BlockSpec(memory_space=pltpu.SMEM)
    vmem = pl.BlockSpec(memory_space=pltpu.VMEM)
    return pl.pallas_call(
        prepare_kernel,
        out_shape=(
            jax.ShapeDtypeStruct((2 * RIM, 3 * WIDE), jnp.bfloat16),
            jax.ShapeDtypeStruct((2 * RIM, 3 * WIDE), jnp.bfloat16),
            jax.ShapeDtypeStruct((3 * DEPTH, DEPTH), jnp.bfloat16),
            jax.ShapeDtypeStruct((3 * DEPTH, DEPTH), jnp.bfloat16),
            jax.ShapeDtypeStruct((2, SIDE, DEPTH), jnp.float32),
        ),
        in_specs=[smem] * 5,
        out_specs=(vmem,) * 5,
        cost_estimate=pl.CostEstimate(flops=1000000, bytes_accessed=1000000, transcendentals=0),
    )(smooth, slope, band, step, edges)


def fill_extended(extended, edges, own, x_even, x_odd, y_even, y_odd, c_even, c_odd):
    high = SIDE + REACH
    low = WIDE - REACH
    x_places = (jnp.where(edges[4] == 0, SIDE, low), jnp.where(edges[4] == 0, low, SIDE))
    y_places = (
        jnp.where(edges[5] == 0, SIDE, WIDE - SLAB), jnp.where(edges[5] == 0, WIDE - SLAB, SIDE)
    )
    extended[0:SIDE, 0:SIDE, :] = own
    extended[high:low, :, :] = jnp.zeros((low - high, WIDE, DEPTH), jnp.float32)
    for place, part in zip(x_places, (x_even, x_odd)):
        extended[pl.ds(place, REACH), 0:SIDE, :] = part
    for place, part, corner in zip(y_places, (y_even, y_odd), (c_even, c_odd)):
        columns = pl.ds(pl.multiple_of(place, SLAB), SLAB)
        extended[0:SIDE, columns, :] = part
        for at, row in enumerate(x_places):
            extended[pl.ds(row, REACH), columns, :] = corner[at * REACH : (at + 1) * REACH]


def stacked_parts(value):
    high, low = split_rows(value)
    return jnp.concatenate([high, low, high], axis=0)


def lane_parts(value):
    high, low = split_rows(value)
    return jnp.concatenate([high, low, high], axis=1)


def take_place(block, place):
    outer, inner, depth = block.shape
    return block.reshape(outer * inner, depth)[pl.ds(place, outer, stride=inner), :]


def along_x_stage(extended, crossed, matrix):
    rows = matrix.shape[0]
    crossed[SIDE + REACH : WIDE - REACH, :, :] = jnp.zeros(
        (WIDE - 2 * REACH - SIDE, rows, DEPTH), jnp.float32
    )
    for pair in range(0, len(IN_COORDS), 2):
        places = IN_COORDS[pair : pair + 2]
        value = jnp.concatenate([take_place(extended, y) for y in places], axis=1)
        out = jnp.dot(matrix, stacked_parts(value), preferred_element_type=jnp.float32)
        for at, y in enumerate(places):
            crossed[y, :, :] = out[:, at * DEPTH : (at + 1) * DEPTH]


def gradient_stages(extended, along_x, along_y, depth_s, depth_g, crossed, flat_s, flat_g, normals, lengths):
    along_x_stage(extended, crossed, along_x[...])
    matrix = along_y[...]
    for at, row in enumerate(OUT_ROWS):
        value = jnp.concatenate(
            [take_place(crossed, row + kind * RIM) for kind in range(2)], axis=1
        )
        got = jnp.dot(matrix, stacked_parts(value), preferred_element_type=jnp.float32)
        flat_s[at, 0:RIM, :] = got[0:RIM, DEPTH:]
        flat_s[at, RIM:, :] = got[RIM:, :DEPTH]
        flat_g[at, :, :] = got[0:RIM, :DEPTH]
    weights_s = depth_s[...]
    weights_g = depth_g[...]
    for at in range(0, SIDE + 2, 2):
        cross = jnp.dot(
            lane_parts(flat_s[at : at + 2].reshape(4 * RIM, DEPTH)), weights_s,
            preferred_element_type=jnp.float32,
        )
        deep = jnp.dot(
            lane_parts(flat_g[at : at + 2].reshape(2 * RIM, DEPTH)), weights_g,
            preferred_element_type=jnp.float32,
        )
        for half in range(2):
            grad_x = cross[2 * half * RIM : (2 * half + 1) * RIM]
            grad_y = cross[(2 * half + 1) * RIM : (2 * half + 2) * RIM]
            grad_z = deep[half * RIM : (half + 1) * RIM]
            square = grad_x * grad_x + grad_y * grad_y + grad_z * grad_z + 1.0
            inverse = lax.rsqrt(square)
            normals[0, at + half, :, :] = grad_x * inverse
            normals[1, at + half, :, :] = grad_y * inverse
            normals[2, at + half, :, :] = grad_z * inverse
            lengths[at + half, :, :] = square * inverse


def advance(own, speed, gain, normals, lengths, out):
    lane = lax.broadcasted_iota(jnp.int32, (SIDE, DEPTH), 1)
    for x in range(SIDE):
        at = x + 1
        across = normals[1, at, :, :]
        deep = normals[2, at, 0:SIDE, :]
        bend = normals[0, at + 1, 0:SIDE, :] - normals[0, at - 1, 0:SIDE, :]
        bend += (pltpu.roll(across, RIM - 1, 0) - pltpu.roll(across, 1, 0))[0:SIDE]
        bend += jnp.where(lane < DEPTH - 1, pltpu.roll(deep, DEPTH - 1, 1), 0.0)
        bend -= jnp.where(lane > 0, pltpu.roll(deep, 1, 1), 0.0)
        push = gain[x // (SIDE // 2)] * lengths[at, 0:SIDE, :]
        out[x, :, :] = own[x, :, :] - push * (speed[x, :, :] - 0.25 * bend)


def speed_stages(extended, along_x, along_y, depth_s, crossed, flat_s, velocity, out):
    along_x_stage(extended, crossed, along_x[0 : RIM + 8, :])
    matrix = along_y[0 : RIM + 8, :]
    for pair in range(0, len(OUT_ROWS), 2):
        value = jnp.concatenate(
            [take_place(crossed, row) for row in OUT_ROWS[pair : pair + 2]], axis=1
        )
        got = jnp.dot(matrix, stacked_parts(value), preferred_element_type=jnp.float32)
        for half in range(2):
            flat_s[pair + half, :, :] = got[0:RIM, half * DEPTH : (half + 1) * DEPTH]
    weights = depth_s[...]
    for at in range(0, SIDE + 2, 2):
        got = jnp.dot(
            lane_parts(flat_s[at : at + 2].reshape(2 * RIM, DEPTH)), weights,
            preferred_element_type=jnp.float32,
        )
        velocity[at : at + 2, :, :] = got.reshape(2, RIM, DEPTH)
    lane = lax.broadcasted_iota(jnp.int32, (SIDE, DEPTH), 1)
    for x in range(SIDE):
        at = x + 1
        rim = velocity[at, :, :]
        centre = rim[0:SIDE]
        total = centre + velocity[at + 1, 0:SIDE, :] + velocity[at - 1, 0:SIDE, :]
        total += (pltpu.roll(rim, RIM - 1, 0) + pltpu.roll(rim, 1, 0))[0:SIDE]
        total += jnp.where(lane < DEPTH - 1, pltpu.roll(centre, DEPTH - 1, 1), 0.0)
        total += jnp.where(lane > 0, pltpu.roll(centre, 1, 1), 0.0)
        out[x, :, :] = total / 7.0


HALOS = 6


def first_kernel(edges, own_s, own, *refs):
    halos = refs[:HALOS]
    along_x, along_y, depth_s, depth_g, gain, out, speed = refs[HALOS : HALOS + 7]
    extended_s, crossed_s, flat_v, velocity = refs[HALOS + 7 : HALOS + 11]
    extended, crossed, flat_s, flat_g, normals, lengths = refs[HALOS + 11 :]
    fill_extended(extended_s, edges, own_s[...], *[halo[0] for halo in halos])
    fill_extended(extended, edges, own[...], *[halo[1] for halo in halos])
    speed_stages(extended_s, along_x, along_y, depth_s, crossed_s, flat_v, velocity, speed)
    gradient_stages(
        extended, along_x, along_y, depth_s, depth_g, crossed, flat_s, flat_g, normals, lengths
    )
    advance(own, speed, gain, normals, lengths, out)


def later_kernel(edges, own, *refs):
    halos = refs[:HALOS]
    along_x, along_y, depth_s, depth_g, gain, speed, out = refs[HALOS : HALOS + 7]
    extended, crossed, flat_s, flat_g, normals, lengths = refs[HALOS + 7 :]
    fill_extended(extended, edges, own[...], *[halo[...] for halo in halos])
    gradient_stages(
        extended, along_x, along_y, depth_s, depth_g, crossed, flat_s, flat_g, normals, lengths
    )
    advance(own, speed, gain, normals, lengths, out)


def call_kernel(body, edges, arrays, outputs, scratch):
    smem = pl.BlockSpec(memory_space=pltpu.SMEM)
    vmem = pl.BlockSpec(memory_space=pltpu.VMEM)
    shape = jax.ShapeDtypeStruct((SIDE, SIDE, DEPTH), jnp.float32)
    return pl.pallas_call(
        body,
        out_shape=(shape,) * outputs,
        in_specs=[smem] + [vmem] * len(arrays),
        out_specs=(vmem,) * outputs,
        scratch_shapes=[pltpu.VMEM(shape, jnp.float32) for shape in scratch],
        compiler_params=pltpu.CompilerParams(vmem_limit_bytes=48 * 1024 * 1024),
    )(edges, *arrays)


def swap(block, axis, first):
    pairs = []
    for low in range(first, lax.axis_size(axis) - 1, 2):
        pairs += [(low, low + 1), (low + 1, low)]
    return lax.ppermute(block, axis, pairs)


def side_pieces(blocks, dim, width, parity):
    even, odd = [], []
    for block in blocks:
        length = block.shape[dim]
        even.append(
            lax.dynamic_slice_in_dim(block, jnp.where(parity == 0, length - width, 0), width, dim)
        )
        odd.append(
            lax.dynamic_slice_in_dim(block, jnp.where(parity == 0, 0, length - width), width, dim)
        )
    if len(blocks) == 1:
        return even[0], odd[0]
    return jnp.stack(even), jnp.stack(odd)


def gather_halos(blocks, parity_x, parity_y):
    even, odd = side_pieces(blocks, 0, REACH, parity_x)
    x_even = swap(even, "gx", 0)
    x_odd = swap(odd, "gx", 1)
    even, odd = side_pieces(blocks, 1, SLAB, parity_y)
    y_even = swap(even, "gy", 0)
    y_odd = swap(odd, "gy", 1)
    edge = jnp.concatenate([x_even, x_odd], axis=-3)
    even, odd = side_pieces([edge], edge.ndim - 2, SLAB, parity_y)
    return x_even, x_odd, y_even, y_odd, swap(even, "gy", 0), swap(odd, "gy", 1)


def per_device(level_set, sensitivity, smooth_taps, slope_taps, band, time_step):
    edges, parity = [], []
    for axis in ("gx", "gy"):
        at = lax.axis_index(axis)
        edges += [at > 0, at < lax.axis_size(axis) - 1]
        parity.append(at & 1)
    edges = jnp.stack([jnp.int32(e) for e in edges] + parity)
    along_x, along_y, depth_s, depth_g, gain = prepare(
        smooth_taps, slope_taps, band, time_step, edges
    )
    matrices = (along_x, along_y, depth_s, depth_g, gain)
    rim = SIDE + 2
    gradient_scratch = [
        (WIDE, WIDE, DEPTH), (WIDE, 2 * RIM, DEPTH), (rim, 2 * RIM, DEPTH),
        (rim, RIM, DEPTH), (3, rim, RIM, DEPTH), (rim, RIM, DEPTH),
    ]
    speed_scratch = [
        (WIDE, WIDE, DEPTH), (WIDE, RIM + 8, DEPTH), (rim, RIM, DEPTH), (rim, RIM, DEPTH)
    ]
    halos = gather_halos([sensitivity, level_set], *parity)
    phi, speed = call_kernel(
        first_kernel, edges, (sensitivity, level_set, *halos, *matrices), 2,
        speed_scratch + gradient_scratch,
    )
    for _ in range(1, UPDATES):
        halos = gather_halos([phi], *parity)
        (phi,) = call_kernel(
            later_kernel, edges, (phi, *halos, *matrices, speed), 1, gradient_scratch
        )
    return phi


def solution(mesh):
    return jax.shard_map(
        per_device,
        mesh=mesh,
        in_specs=(P("gx", "gy", None), P("gx", "gy", None), P(), P(), P("gx", "gy", None), P()),
        out_specs=P("gx", "gy", None),
        check_vma=False,
    )
```

```python
import functools

import jax
import jax.numpy as jnp
from jax import lax
from jax.experimental import pallas as pl
from jax.experimental.pallas import tpu as pltpu
from jax.sharding import PartitionSpec as P

UPDATES = 2
REACH = 13
SLAB = 16
SIDE = 32
RIM = 40
WIDE = 64
DEPTH = 128
TAPS = 25

OUT_ROWS = [RIM - 1] + list(range(SIDE + 1))


def split_rows(value):
    high = value.astype(jnp.bfloat16)
    low = (value - high.astype(jnp.float32)).astype(jnp.bfloat16)
    return high, low


def tap_select(index, taps):
    total = jnp.zeros(index.shape, jnp.float32)
    for k in range(TAPS):
        total = jnp.where(index == k, taps[k], total)
    return total


def side_matrix(axis, smooth, slope):
    at = lax.axis_index(axis)
    last = lax.axis_size(axis) - 1
    shape = (RIM, 3 * WIDE)
    row = lax.broadcasted_iota(jnp.int32, shape, 0)
    column = lax.broadcasted_iota(jnp.int32, shape, 1)
    place = column & (WIDE - 1)
    width = REACH if axis == "gx" else SLAB
    source = place
    for slot, side in ((0, at & 1), (1, 1 - (at & 1))):
        start = SIDE + slot * SLAB
        moved = place - start + jnp.where(side == 0, SIDE, -width)
        source = jnp.where((place >= start) & (place < start + SLAB), moved, source)
        source = jnp.where((place >= start + width) & (place < start + SLAB), -WIDE, source)
    target = jnp.where(row < RIM - 1, row, -1)
    index = source - target + TAPS // 2
    inside = (row < SIDE) | ((row == SIDE) & (at < last)) | ((row == RIM - 1) & (at > 0))
    index = jnp.where(inside, index, -1)
    parts = []
    for taps in (smooth, slope):
        full = tap_select(index, taps)
        high = full.astype(jnp.bfloat16).astype(jnp.float32)
        parts.append(jnp.where(column < 2 * WIDE, high, full - high))
    return jnp.concatenate(parts, axis=0).astype(jnp.bfloat16)


def block_gain(band, step, p):
    blocks_y, blocks_z = 2, 4
    rows = SIDE // blocks_y
    lane = lax.broadcasted_iota(jnp.int32, (rows, DEPTH), 1) // (DEPTH // blocks_z)
    parts = []
    for q in range(blocks_y):
        value = jnp.zeros(lane.shape, jnp.float32)
        for r in range(blocks_z):
            entry = band[p, q, r].astype(jnp.float32) * step[0]
            value = jnp.where(lane == r, entry, value)
        parts.append(value)
    return jnp.concatenate(parts, axis=0)


def prepare_kernel(smooth, slope, band, step, out, gain):
    for p in range(2):
        gain[p, :, :] = block_gain(band, step, p)
    for at, axis in enumerate(("gx", "gy")):
        out[2 * at * RIM : 2 * (at + 1) * RIM, 0 : 3 * WIDE] = side_matrix(axis, smooth, slope)
        out[2 * at * RIM : 2 * (at + 1) * RIM, 3 * WIDE :] = jnp.zeros((2 * RIM, WIDE), jnp.bfloat16)
    shape = (DEPTH, DEPTH)
    index = (
        lax.broadcasted_iota(jnp.int32, shape, 0)
        - lax.broadcasted_iota(jnp.int32, shape, 1)
        + TAPS // 2
    )
    for at, taps in enumerate((smooth, slope)):
        columns = slice(at * DEPTH, (at + 1) * DEPTH)
        high, low = split_rows(tap_select(index, taps))
        out[4 * RIM : 4 * RIM + DEPTH, columns] = high
        out[4 * RIM + DEPTH : 4 * RIM + 2 * DEPTH, columns] = high
        out[4 * RIM + 2 * DEPTH :, columns] = low


SMEM = pl.BlockSpec(memory_space=pltpu.SMEM)
VMEM = pl.BlockSpec(memory_space=pltpu.VMEM)
SMALL = pltpu.CompilerParams(vmem_limit_bytes=4 * 1024 * 1024)


def prepare(smooth, slope, band, step):
    return pl.pallas_call(
        prepare_kernel,
        out_shape=(
            jax.ShapeDtypeStruct((4 * RIM + 3 * DEPTH, 2 * DEPTH), jnp.bfloat16),
            jax.ShapeDtypeStruct((2, SIDE, DEPTH), jnp.float32),
        ),
        in_specs=[SMEM] * 4,
        out_specs=(VMEM, VMEM),
        compiler_params=SMALL,
        cost_estimate=pl.CostEstimate(flops=1000000, bytes_accessed=1000000, transcendentals=0),
    )(smooth, slope, band, step)


def along_matrix(matrices, axis, rows):
    return matrices[2 * axis * RIM : 2 * axis * RIM + rows, 0 : 3 * WIDE]


def depth_matrix(matrices, kind):
    return matrices[4 * RIM :, kind * DEPTH : (kind + 1) * DEPTH]


def fill_extended(extended, own, x_even, x_odd, y_even, y_odd, c_even, c_odd):
    extended[0:SIDE, 0:SIDE, :] = own
    gap = jnp.zeros((SLAB - REACH, WIDE, DEPTH), jnp.float32)
    for at, part in enumerate((x_even, x_odd)):
        start = SIDE + at * SLAB
        extended[start : start + REACH, 0:SIDE, :] = part
        extended[start + REACH : start + SLAB, :, :] = gap
    for at, (part, corner) in enumerate(((y_even, c_even), (y_odd, c_odd))):
        columns = slice(SIDE + at * SLAB, SIDE + (at + 1) * SLAB)
        extended[0:SIDE, columns, :] = part
        for side in range(2):
            start = SIDE + side * SLAB
            extended[start : start + REACH, columns, :] = corner[side * REACH : (side + 1) * REACH]


def stacked_parts(value):
    high, low = split_rows(value)
    return jnp.concatenate([high, low, high], axis=0)


def lane_parts(value):
    high, low = split_rows(value)
    return jnp.concatenate([high, low, high], axis=1)


def take_place(block, place):
    outer, inner, depth = block.shape
    return block.reshape(outer * inner, depth)[pl.ds(place, outer, stride=inner), :]


def along_x_stage(extended, crossed, matrix):
    for pair in range(0, WIDE, 2):
        places = (pair, pair + 1)
        value = jnp.concatenate([take_place(extended, y) for y in places], axis=1)
        out = jnp.dot(matrix, stacked_parts(value), preferred_element_type=jnp.float32)
        for at, y in enumerate(places):
            crossed[y, :, :] = out[:, at * DEPTH : (at + 1) * DEPTH]


def gradient_stages(extended, matrices, crossed, flat_s, flat_g, normals, lengths):
    along_x_stage(extended, crossed, along_matrix(matrices, 0, 2 * RIM))
    matrix = along_matrix(matrices, 1, 2 * RIM)
    for at, row in enumerate(OUT_ROWS):
        value = jnp.concatenate(
            [take_place(crossed, row + kind * RIM) for kind in range(2)], axis=1
        )
        got = jnp.dot(matrix, stacked_parts(value), preferred_element_type=jnp.float32)
        flat_s[at, 0:RIM, :] = got[0:RIM, DEPTH:]
        flat_s[at, RIM:, :] = got[RIM:, :DEPTH]
        flat_g[at, :, :] = got[0:RIM, :DEPTH]
    weights_s = depth_matrix(matrices, 0)
    weights_g = depth_matrix(matrices, 1)
    for at in range(0, SIDE + 2, 2):
        cross = jnp.dot(
            lane_parts(flat_s[at : at + 2].reshape(4 * RIM, DEPTH)), weights_s,
            preferred_element_type=jnp.float32,
        )
        deep = jnp.dot(
            lane_parts(flat_g[at : at + 2].reshape(2 * RIM, DEPTH)), weights_g,
            preferred_element_type=jnp.float32,
        )
        for half in range(2):
            grad_x = cross[2 * half * RIM : (2 * half + 1) * RIM]
            grad_y = cross[(2 * half + 1) * RIM : (2 * half + 2) * RIM]
            grad_z = deep[half * RIM : (half + 1) * RIM]
            square = grad_x * grad_x + grad_y * grad_y + grad_z * grad_z + 1.0
            inverse = lax.rsqrt(square)
            normals[0, at + half, :, :] = grad_x * inverse
            normals[1, at + half, :, :] = grad_y * inverse
            normals[2, at + half, :, :] = grad_z * inverse
            lengths[at + half, :, :] = square * inverse


def advance(own, speed, gain, normals, lengths, out):
    lane = lax.broadcasted_iota(jnp.int32, (SIDE, DEPTH), 1)
    for x in range(SIDE):
        at = x + 1
        across = normals[1, at, :, :]
        deep = normals[2, at, 0:SIDE, :]
        bend = normals[0, at + 1, 0:SIDE, :] - normals[0, at - 1, 0:SIDE, :]
        bend += (pltpu.roll(across, RIM - 1, 0) - pltpu.roll(across, 1, 0))[0:SIDE]
        bend += jnp.where(lane < DEPTH - 1, pltpu.roll(deep, DEPTH - 1, 1), 0.0)
        bend -= jnp.where(lane > 0, pltpu.roll(deep, 1, 1), 0.0)
        push = gain[x // (SIDE // 2), :, :] * lengths[at, 0:SIDE, :]
        out[x, :, :] = own[x, :, :] - push * (speed[x, :, :] - 0.25 * bend)


def speed_stages(extended, matrices, crossed, flat_s, velocity, out):
    along_x_stage(extended, crossed, along_matrix(matrices, 0, RIM + 8))
    matrix = along_matrix(matrices, 1, RIM + 8)
    for pair in range(0, len(OUT_ROWS), 2):
        value = jnp.concatenate(
            [take_place(crossed, row) for row in OUT_ROWS[pair : pair + 2]], axis=1
        )
        got = jnp.dot(matrix, stacked_parts(value), preferred_element_type=jnp.float32)
        for half in range(2):
            flat_s[pair + half, :, :] = got[0:RIM, half * DEPTH : (half + 1) * DEPTH]
    weights = depth_matrix(matrices, 0)
    for at in range(0, SIDE + 2, 2):
        got = jnp.dot(
            lane_parts(flat_s[at : at + 2].reshape(2 * RIM, DEPTH)), weights,
            preferred_element_type=jnp.float32,
        )
        velocity[at : at + 2, :, :] = got.reshape(2, RIM, DEPTH)
    lane = lax.broadcasted_iota(jnp.int32, (SIDE, DEPTH), 1)
    for x in range(SIDE):
        at = x + 1
        rim = velocity[at, :, :]
        centre = rim[0:SIDE]
        total = centre + velocity[at + 1, 0:SIDE, :] + velocity[at - 1, 0:SIDE, :]
        total += (pltpu.roll(rim, RIM - 1, 0) + pltpu.roll(rim, 1, 0))[0:SIDE]
        total += jnp.where(lane < DEPTH - 1, pltpu.roll(centre, DEPTH - 1, 1), 0.0)
        total += jnp.where(lane > 0, pltpu.roll(centre, 1, 1), 0.0)
        out[x, :, :] = total / 7.0


HALOS = 6


def first_kernel(own_s, own, *refs):
    halos = refs[:HALOS]
    matrices, gain, out, speed = refs[HALOS : HALOS + 4]
    extended_s, crossed_s, flat_v, velocity = refs[HALOS + 4 : HALOS + 8]
    extended, crossed, flat_s, flat_g, normals, lengths = refs[HALOS + 8 :]
    fill_extended(extended_s, own_s[...], *[halo[0] for halo in halos])
    fill_extended(extended, own[...], *[halo[1] for halo in halos])
    speed_stages(extended_s, matrices, crossed_s, flat_v, velocity, speed)
    gradient_stages(extended, matrices, crossed, flat_s, flat_g, normals, lengths)
    advance(own, speed, gain, normals, lengths, out)


def later_kernel(own, *refs):
    halos = refs[:HALOS]
    matrices, gain, speed, out = refs[HALOS : HALOS + 4]
    extended, crossed, flat_s, flat_g, normals, lengths = refs[HALOS + 4 :]
    fill_extended(extended, own[...], *[halo[...] for halo in halos])
    gradient_stages(extended, matrices, crossed, flat_s, flat_g, normals, lengths)
    advance(own, speed, gain, normals, lengths, out)


def call_kernel(body, arrays, outputs, scratch):
    shape = jax.ShapeDtypeStruct((SIDE, SIDE, DEPTH), jnp.float32)
    return pl.pallas_call(
        body,
        out_shape=(shape,) * outputs,
        in_specs=[VMEM] * len(arrays),
        out_specs=(VMEM,) * outputs,
        scratch_shapes=[pltpu.VMEM(shape, jnp.float32) for shape in scratch],
        compiler_params=pltpu.CompilerParams(vmem_limit_bytes=20 * 1024 * 1024),
    )(*arrays)


def corner_kernel(x_even, x_odd, even, odd):
    parity = lax.axis_index("gy") & 1
    for side, target in enumerate((even, odd)):
        start = pl.multiple_of(jnp.where(parity == side, SIDE - SLAB, 0), SLAB)
        for at, source in enumerate((x_even, x_odd)):
            target[..., at * REACH : (at + 1) * REACH, :, :] = source[..., pl.ds(start, SLAB), :]


def corner_sides(x_halos):
    shape = x_halos[0].shape[:-3] + (2 * REACH, SLAB, DEPTH)
    out = jax.ShapeDtypeStruct(shape, jnp.float32)
    return pl.pallas_call(
        corner_kernel,
        out_shape=(out, out),
        in_specs=[VMEM] * 2,
        out_specs=(VMEM, VMEM),
        compiler_params=SMALL,
    )(*x_halos)


def swap(block, axis, first):
    pairs = []
    for low in range(first, lax.axis_size(axis) - 1, 2):
        pairs += [(low, low + 1), (low + 1, low)]
    return lax.ppermute(block, axis, pairs)


def both_sides(block, dim, width, parity):
    length = block.shape[dim]
    high = jnp.where(parity == 0, length - width, 0)
    return (
        lax.dynamic_slice_in_dim(block, high, width, dim),
        lax.dynamic_slice_in_dim(block, length - width - high, width, dim),
    )


def stacked_sides(blocks, dim, width, parity):
    return [jnp.stack(side) for side in zip(*[both_sides(b, dim, width, parity) for b in blocks])]


def swap_sides(pieces, axis):
    return swap(pieces[0], axis, 0), swap(pieces[1], axis, 1)


def per_device(level_set, sensitivity, smooth_taps, slope_taps, band, time_step):
    parity = [lax.axis_index(axis) & 1 for axis in ("gx", "gy")]
    fields = [sensitivity, level_set]
    x_halos = swap_sides(stacked_sides(fields, 0, REACH, parity[0]), "gx")
    y_halos = swap_sides(stacked_sides(fields, 1, SLAB, parity[1]), "gy")
    matrices = prepare(smooth_taps, slope_taps, band, time_step)
    x_halos, matrices = lax.optimization_barrier((x_halos, matrices))
    corners = swap_sides(corner_sides(x_halos), "gy")
    rim = SIDE + 2
    gradient_scratch = [
        (WIDE, WIDE, DEPTH), (WIDE, 2 * RIM, DEPTH), (rim, 2 * RIM, DEPTH),
        (rim, RIM, DEPTH), (3, rim, RIM, DEPTH), (rim, RIM, DEPTH),
    ]
    speed_scratch = [
        (WIDE, WIDE, DEPTH), (WIDE, RIM + 8, DEPTH), (rim, RIM, DEPTH), (rim, RIM, DEPTH)
    ]
    phi, speed = call_kernel(
        first_kernel, (*fields, *x_halos, *y_halos, *corners, *matrices), 2,
        speed_scratch + gradient_scratch,
    )
    for _ in range(1, UPDATES):
        x_halos = swap_sides(both_sides(phi, 0, REACH, parity[0]), "gx")
        y_halos = swap_sides(both_sides(phi, 1, SLAB, parity[1]), "gy")
        corners = swap_sides(corner_sides(x_halos), "gy")
        (phi,) = call_kernel(
            later_kernel, (phi, *x_halos, *y_halos, *corners, *matrices, speed), 1, gradient_scratch,
        )
    return phi


def solution(mesh):
    return jax.shard_map(
        per_device,
        mesh=mesh,
        in_specs=(P("gx", "gy", None), P("gx", "gy", None), P(), P(), P("gx", "gy", None), P()),
        out_specs=P("gx", "gy", None),
        check_vma=False,
    )
```

```python
import functools

import jax
import jax.numpy as jnp
from jax import lax
from jax.experimental import pallas as pl
from jax.experimental.pallas import tpu as pltpu
from jax.sharding import PartitionSpec as P

UPDATES = 2
REACH = 13
SLAB = 16
SIDE = 32
RIM = 40
WIDE = 64
DEPTH = 128
TAPS = 25

OUT_ROWS = [RIM - 1] + list(range(SIDE + 1))


def split_rows(value):
    high = value.astype(jnp.bfloat16)
    low = (value - high.astype(jnp.float32)).astype(jnp.bfloat16)
    return high, low


def tap_select(index, taps):
    total = jnp.zeros(index.shape, jnp.float32)
    for k in range(TAPS):
        total = jnp.where(index == k, taps[k], total)
    return total


def side_matrix(axis, smooth, slope):
    at = lax.axis_index(axis)
    last = lax.axis_size(axis) - 1
    shape = (RIM, 3 * WIDE)
    row = lax.broadcasted_iota(jnp.int32, shape, 0)
    column = lax.broadcasted_iota(jnp.int32, shape, 1)
    place = column & (WIDE - 1)
    width = REACH if axis == "gx" else SLAB
    source = place
    for slot, side in ((0, at & 1), (1, 1 - (at & 1))):
        start = SIDE + slot * SLAB
        moved = place - start + jnp.where(side == 0, SIDE, -width)
        source = jnp.where((place >= start) & (place < start + SLAB), moved, source)
        source = jnp.where((place >= start + width) & (place < start + SLAB), -WIDE, source)
    target = jnp.where(row < RIM - 1, row, -1)
    index = source - target + TAPS // 2
    inside = (row < SIDE) | ((row == SIDE) & (at < last)) | ((row == RIM - 1) & (at > 0))
    index = jnp.where(inside, index, -1)
    parts = []
    for taps in (smooth, slope):
        full = tap_select(index, taps)
        high = full.astype(jnp.bfloat16).astype(jnp.float32)
        parts.append(jnp.where(column < 2 * WIDE, high, full - high))
    return jnp.concatenate(parts, axis=0).astype(jnp.bfloat16)


def block_gain(band, step, p):
    blocks_y, blocks_z = 2, 4
    rows = SIDE // blocks_y
    lane = lax.broadcasted_iota(jnp.int32, (rows, DEPTH), 1) // (DEPTH // blocks_z)
    parts = []
    for q in range(blocks_y):
        value = jnp.zeros(lane.shape, jnp.float32)
        for r in range(blocks_z):
            entry = band[p, q, r].astype(jnp.float32) * step[0]
            value = jnp.where(lane == r, entry, value)
        parts.append(value)
    return jnp.concatenate(parts, axis=0)


def prepare_kernel(smooth, slope, band, step, out, gain):
    for p in range(2):
        gain[p, :, :] = block_gain(band, step, p)
    for at, axis in enumerate(("gx", "gy")):
        out[2 * at * RIM : 2 * (at + 1) * RIM, 0 : 3 * WIDE] = side_matrix(axis, smooth, slope)
        out[2 * at * RIM : 2 * (at + 1) * RIM, 3 * WIDE :] = jnp.zeros((2 * RIM, WIDE), jnp.bfloat16)
    shape = (DEPTH, DEPTH)
    index = (
        lax.broadcasted_iota(jnp.int32, shape, 0)
        - lax.broadcasted_iota(jnp.int32, shape, 1)
        + TAPS // 2
    )
    for at, taps in enumerate((smooth, slope)):
        columns = slice(at * DEPTH, (at + 1) * DEPTH)
        high, low = split_rows(tap_select(index, taps))
        out[4 * RIM : 4 * RIM + DEPTH, columns] = high
        out[4 * RIM + DEPTH : 4 * RIM + 2 * DEPTH, columns] = high
        out[4 * RIM + 2 * DEPTH :, columns] = low


SMEM = pl.BlockSpec(memory_space=pltpu.SMEM)
VMEM = pl.BlockSpec(memory_space=pltpu.VMEM)
SMALL = pltpu.CompilerParams(vmem_limit_bytes=4 * 1024 * 1024)


def prepare(smooth, slope, band, step):
    return pl.pallas_call(
        prepare_kernel,
        out_shape=(
            jax.ShapeDtypeStruct((4 * RIM + 3 * DEPTH, 2 * DEPTH), jnp.bfloat16),
            jax.ShapeDtypeStruct((2, SIDE, DEPTH), jnp.float32),
        ),
        in_specs=[SMEM] * 4,
        out_specs=(VMEM, VMEM),
        compiler_params=SMALL,
        cost_estimate=pl.CostEstimate(flops=1000000, bytes_accessed=1000000, transcendentals=0),
    )(smooth, slope, band, step)


def along_matrix(matrices, axis, rows):
    return matrices[2 * axis * RIM : 2 * axis * RIM + rows, 0 : 3 * WIDE]


def depth_matrix(matrices, kind):
    return matrices[4 * RIM :, kind * DEPTH : (kind + 1) * DEPTH]


def fill_extended(extended, own, x_even, x_odd, y_even, y_odd, c_even, c_odd):
    extended[0:SIDE, 0:SIDE, :] = own
    gap = jnp.zeros((SLAB - REACH, WIDE, DEPTH), jnp.float32)
    for at, part in enumerate((x_even, x_odd)):
        start = SIDE + at * SLAB
        extended[start : start + REACH, 0:SIDE, :] = part
        extended[start + REACH : start + SLAB, 0:WIDE, :] = gap
    for at, (part, corner) in enumerate(((y_even, c_even), (y_odd, c_odd))):
        columns = slice(SIDE + at * SLAB, SIDE + (at + 1) * SLAB)
        extended[0:SIDE, columns, :] = part
        for side in range(2):
            start = SIDE + side * SLAB
            extended[start : start + REACH, columns, :] = corner[side * REACH : (side + 1) * REACH]


def stacked_parts(value):
    high, low = split_rows(value)
    return jnp.concatenate([high, low, high], axis=0)


def lane_parts(value):
    high, low = split_rows(value)
    return jnp.concatenate([high, low, high], axis=1)


def take_place(block, place):
    outer, inner, depth = block.shape
    return block.reshape(outer * inner, depth)[pl.ds(place, outer, stride=inner), :]


def along_x_stage(extended, crossed, matrix):
    for pair in range(0, WIDE, 2):
        places = (pair, pair + 1)
        value = jnp.concatenate([take_place(extended, y) for y in places], axis=1)
        out = jnp.dot(matrix, stacked_parts(value), preferred_element_type=jnp.float32)
        for at, y in enumerate(places):
            crossed[y, 0 : out.shape[0], :] = out[:, at * DEPTH : (at + 1) * DEPTH]


def gradient_stages(extended, matrices, crossed, flat_s, flat_g, normals, lengths, finish):
    along_x_stage(extended, crossed, along_matrix(matrices, 0, 2 * RIM))
    matrix = along_matrix(matrices, 1, 2 * RIM)
    for at, row in enumerate(OUT_ROWS):
        value = jnp.concatenate(
            [take_place(crossed, row + kind * RIM) for kind in range(2)], axis=1
        )
        got = jnp.dot(matrix, stacked_parts(value), preferred_element_type=jnp.float32)
        flat_s[at, 0:RIM, :] = got[0:RIM, DEPTH:]
        flat_s[at, RIM:, :] = got[RIM:, :DEPTH]
        flat_g[at, :, :] = got[0:RIM, :DEPTH]
    weights_s = depth_matrix(matrices, 0)
    weights_g = depth_matrix(matrices, 1)
    for at in range(0, SIDE + 2, 2):
        cross = jnp.dot(
            lane_parts(flat_s[at : at + 2].reshape(4 * RIM, DEPTH)), weights_s,
            preferred_element_type=jnp.float32,
        )
        deep = jnp.dot(
            lane_parts(flat_g[at : at + 2].reshape(2 * RIM, DEPTH)), weights_g,
            preferred_element_type=jnp.float32,
        )
        for half in range(2):
            grad_x = cross[2 * half * RIM : (2 * half + 1) * RIM]
            grad_y = cross[(2 * half + 1) * RIM : (2 * half + 2) * RIM]
            grad_z = deep[half * RIM : (half + 1) * RIM]
            square = grad_x * grad_x + grad_y * grad_y + grad_z * grad_z + 1.0
            inverse = lax.rsqrt(square)
            normals[0, at + half, :, :] = grad_x * inverse
            normals[1, at + half, :, :] = grad_y * inverse
            normals[2, at + half, :, :] = grad_z * inverse
            lengths[at + half, :, :] = square * inverse
        if at > 0:
            finish(at - 2)
            finish(at - 1)


def advance(x, own, speed, gain, normals, lengths):
    lane = lax.broadcasted_iota(jnp.int32, (SIDE, DEPTH), 1)
    at = x + 1
    across = normals[1, at, :, :]
    deep = normals[2, at, 0:SIDE, :]
    bend = normals[0, at + 1, 0:SIDE, :] - normals[0, at - 1, 0:SIDE, :]
    bend += (pltpu.roll(across, RIM - 1, 0) - pltpu.roll(across, 1, 0))[0:SIDE]
    bend += jnp.where(lane < DEPTH - 1, pltpu.roll(deep, DEPTH - 1, 1), 0.0)
    bend -= jnp.where(lane > 0, pltpu.roll(deep, 1, 1), 0.0)
    push = gain[x // (SIDE // 2), :, :] * lengths[at, 0:SIDE, :]
    return own[x, :, :] - push * (speed[x, :, :] - 0.25 * bend)


def speed_stages(extended, matrices, crossed, flat_s, velocity, out):
    along_x_stage(extended, crossed, along_matrix(matrices, 0, RIM + 8))
    matrix = along_matrix(matrices, 1, RIM + 8)
    for pair in range(0, len(OUT_ROWS), 2):
        value = jnp.concatenate(
            [take_place(crossed, row) for row in OUT_ROWS[pair : pair + 2]], axis=1
        )
        got = jnp.dot(matrix, stacked_parts(value), preferred_element_type=jnp.float32)
        for half in range(2):
            flat_s[pair + half, :, :] = got[0:RIM, half * DEPTH : (half + 1) * DEPTH]
    weights = depth_matrix(matrices, 0)
    for at in range(0, SIDE + 2, 2):
        got = jnp.dot(
            lane_parts(flat_s[at : at + 2].reshape(2 * RIM, DEPTH)), weights,
            preferred_element_type=jnp.float32,
        )
        velocity[at : at + 2, :, :] = got.reshape(2, RIM, DEPTH)
    lane = lax.broadcasted_iota(jnp.int32, (SIDE, DEPTH), 1)
    for x in range(SIDE):
        at = x + 1
        rim = velocity[at, :, :]
        centre = rim[0:SIDE]
        total = centre + velocity[at + 1, 0:SIDE, :] + velocity[at - 1, 0:SIDE, :]
        total += (pltpu.roll(rim, RIM - 1, 0) + pltpu.roll(rim, 1, 0))[0:SIDE]
        total += jnp.where(lane < DEPTH - 1, pltpu.roll(centre, DEPTH - 1, 1), 0.0)
        total += jnp.where(lane > 0, pltpu.roll(centre, 1, 1), 0.0)
        out[x, :, :] = total / 7.0


HALOS = 6


def first_kernel(own_s, own, *refs):
    halos = refs[:HALOS]
    matrices, gain, out, speed = refs[HALOS : HALOS + 4]
    extended_s, crossed_s, flat_v, velocity = refs[HALOS + 4 : HALOS + 8]
    extended, crossed, flat_s, flat_g, normals, lengths = refs[HALOS + 8 :]
    fill_extended(extended_s, own_s[...], *[halo[0] for halo in halos])
    fill_extended(extended, own[...], *[halo[1] for halo in halos])
    speed_stages(extended_s, matrices, crossed_s, flat_v, velocity, speed)

    def finish(x):
        out[x, :, :] = advance(x, own, speed, gain, normals, lengths)

    gradient_stages(extended, matrices, crossed, flat_s, flat_g, normals, lengths, finish)


def later_kernel(own, *refs):
    halos = refs[:HALOS]
    matrices, gain, speed, out = refs[HALOS : HALOS + 4]
    extended, crossed, flat_s, flat_g, normals, lengths = refs[HALOS + 4 :]
    fill_extended(extended, own[...], *[halo[...] for halo in halos])

    def finish(x):
        out[x, :, :] = advance(x, own, speed, gain, normals, lengths)

    gradient_stages(extended, matrices, crossed, flat_s, flat_g, normals, lengths, finish)


def call_kernel(body, arrays, outputs, scratch):
    shape = jax.ShapeDtypeStruct((SIDE, SIDE, DEPTH), jnp.float32)
    return pl.pallas_call(
        body,
        out_shape=(shape,) * outputs,
        in_specs=[VMEM] * len(arrays),
        out_specs=(VMEM,) * outputs,
        scratch_shapes=[pltpu.VMEM(shape, jnp.float32) for shape in scratch],
        compiler_params=pltpu.CompilerParams(vmem_limit_bytes=20 * 1024 * 1024),
    )(*arrays)


def corner_kernel(x_even, x_odd, even, odd):
    parity = lax.axis_index("gy") & 1
    for side, target in enumerate((even, odd)):
        start = pl.multiple_of(jnp.where(parity == side, SIDE - SLAB, 0), SLAB)
        for at, source in enumerate((x_even, x_odd)):
            target[..., at * REACH : (at + 1) * REACH, :, :] = source[..., pl.ds(start, SLAB), :]


def corner_sides(x_halos):
    shape = x_halos[0].shape[:-3] + (2 * REACH, SLAB, DEPTH)
    out = jax.ShapeDtypeStruct(shape, jnp.float32)
    return pl.pallas_call(
        corner_kernel,
        out_shape=(out, out),
        in_specs=[VMEM] * 2,
        out_specs=(VMEM, VMEM),
        compiler_params=SMALL,
    )(*x_halos)


def swap(block, axis, first):
    pairs = []
    for low in range(first, lax.axis_size(axis) - 1, 2):
        pairs += [(low, low + 1), (low + 1, low)]
    return lax.ppermute(block, axis, pairs)


def both_sides(block, dim, width, parity):
    length = block.shape[dim]
    high = jnp.where(parity == 0, length - width, 0)
    return (
        lax.dynamic_slice_in_dim(block, high, width, dim),
        lax.dynamic_slice_in_dim(block, length - width - high, width, dim),
    )


def stacked_sides(blocks, dim, width, parity):
    return [jnp.stack(side) for side in zip(*[both_sides(b, dim, width, parity) for b in blocks])]


def swap_sides(pieces, axis):
    return swap(pieces[0], axis, 0), swap(pieces[1], axis, 1)


def per_device(level_set, sensitivity, smooth_taps, slope_taps, band, time_step):
    parity = [lax.axis_index(axis) & 1 for axis in ("gx", "gy")]
    fields = [sensitivity, level_set]
    x_halos = swap_sides(stacked_sides(fields, 0, REACH, parity[0]), "gx")
    y_halos = swap_sides(stacked_sides(fields, 1, SLAB, parity[1]), "gy")
    matrices = prepare(smooth_taps, slope_taps, band, time_step)
    x_halos, matrices = lax.optimization_barrier((x_halos, matrices))
    corners = swap_sides(corner_sides(x_halos), "gy")
    rim = SIDE + 2
    gradient_scratch = [
        (WIDE, WIDE + 8, DEPTH), (WIDE, 2 * RIM + 8, DEPTH), (rim, 2 * RIM, DEPTH),
        (rim, RIM, DEPTH), (3, rim, RIM, DEPTH), (rim, RIM, DEPTH),
    ]
    speed_scratch = [
        (WIDE, WIDE + 8, DEPTH), (WIDE, RIM + 16, DEPTH), (rim, RIM, DEPTH), (rim, RIM, DEPTH)
    ]
    phi, speed = call_kernel(
        first_kernel, (*fields, *x_halos, *y_halos, *corners, *matrices), 2,
        speed_scratch + gradient_scratch,
    )
    for _ in range(1, UPDATES):
        x_halos = swap_sides(both_sides(phi, 0, REACH, parity[0]), "gx")
        y_halos = swap_sides(both_sides(phi, 1, SLAB, parity[1]), "gy")
        corners = swap_sides(corner_sides(x_halos), "gy")
        (phi,) = call_kernel(
            later_kernel, (phi, *x_halos, *y_halos, *corners, *matrices, speed), 1, gradient_scratch,
        )
    return phi


def solution(mesh):
    return jax.shard_map(
        per_device,
        mesh=mesh,
        in_specs=(P("gx", "gy", None), P("gx", "gy", None), P(), P(), P("gx", "gy", None), P()),
        out_specs=P("gx", "gy", None),
        check_vma=False,
    )
```

```python
import functools

import jax
import jax.numpy as jnp
from jax import lax
from jax.experimental import pallas as pl
from jax.experimental.pallas import tpu as pltpu
from jax.sharding import PartitionSpec as P

UPDATES = 2
REACH = 13
SLAB = 16
SIDE = 32
RIM = 40
WIDE = 64
DEPTH = 128
TAPS = 25

OUT_ROWS = [RIM - 1] + list(range(SIDE + 1))


def split_rows(value):
    high = value.astype(jnp.bfloat16)
    low = (value - high.astype(jnp.float32)).astype(jnp.bfloat16)
    return high, low


def tap_select(index, taps):
    total = jnp.zeros(index.shape, jnp.float32)
    for k in range(TAPS):
        total = jnp.where(index == k, taps[k], total)
    return total


def side_matrix(axis, smooth, slope):
    at = lax.axis_index(axis)
    last = lax.axis_size(axis) - 1
    shape = (RIM, 3 * WIDE)
    row = lax.broadcasted_iota(jnp.int32, shape, 0)
    column = lax.broadcasted_iota(jnp.int32, shape, 1)
    place = column & (WIDE - 1)
    width = REACH if axis == "gx" else SLAB
    source = place
    for slot, side in ((0, at & 1), (1, 1 - (at & 1))):
        start = SIDE + slot * SLAB
        moved = place - start + jnp.where(side == 0, SIDE, -width)
        source = jnp.where((place >= start) & (place < start + SLAB), moved, source)
        source = jnp.where((place >= start + width) & (place < start + SLAB), -WIDE, source)
    target = jnp.where(row < RIM - 1, row, -1)
    index = source - target + TAPS // 2
    inside = (row < SIDE) | ((row == SIDE) & (at < last)) | ((row == RIM - 1) & (at > 0))
    index = jnp.where(inside, index, -1)
    parts = []
    for taps in (smooth, slope):
        full = tap_select(index, taps)
        high = full.astype(jnp.bfloat16).astype(jnp.float32)
        parts.append(jnp.where(column < 2 * WIDE, high, full - high))
    return jnp.concatenate(parts, axis=0).astype(jnp.bfloat16)


def block_gain(band, step, p):
    blocks_y, blocks_z = 2, 4
    rows = SIDE // blocks_y
    lane = lax.broadcasted_iota(jnp.int32, (rows, DEPTH), 1) // (DEPTH // blocks_z)
    parts = []
    for q in range(blocks_y):
        value = jnp.zeros(lane.shape, jnp.float32)
        for r in range(blocks_z):
            entry = band[p, q, r].astype(jnp.float32) * step[0]
            value = jnp.where(lane == r, entry, value)
        parts.append(value)
    return jnp.concatenate(parts, axis=0)


def prepare_kernel(smooth, slope, band, step, out, gain):
    for p in range(2):
        gain[p, :, :] = block_gain(band, step, p)
    for at, axis in enumerate(("gx", "gy")):
        out[2 * at * RIM : 2 * (at + 1) * RIM, 0 : 3 * WIDE] = side_matrix(axis, smooth, slope)
        out[2 * at * RIM : 2 * (at + 1) * RIM, 3 * WIDE :] = jnp.zeros((2 * RIM, WIDE), jnp.bfloat16)
    shape = (DEPTH, DEPTH)
    index = (
        lax.broadcasted_iota(jnp.int32, shape, 0)
        - lax.broadcasted_iota(jnp.int32, shape, 1)
        + TAPS // 2
    )
    for at, taps in enumerate((smooth, slope)):
        columns = slice(at * DEPTH, (at + 1) * DEPTH)
        high, low = split_rows(tap_select(index, taps))
        out[4 * RIM : 4 * RIM + DEPTH, columns] = high
        out[4 * RIM + DEPTH : 4 * RIM + 2 * DEPTH, columns] = high
        out[4 * RIM + 2 * DEPTH :, columns] = low


SMEM = pl.BlockSpec(memory_space=pltpu.SMEM)
VMEM = pl.BlockSpec(memory_space=pltpu.VMEM)
SMALL = pltpu.CompilerParams(vmem_limit_bytes=4 * 1024 * 1024)


def prepare(smooth, slope, band, step):
    return pl.pallas_call(
        prepare_kernel,
        out_shape=(
            jax.ShapeDtypeStruct((4 * RIM + 3 * DEPTH, 2 * DEPTH), jnp.bfloat16),
            jax.ShapeDtypeStruct((2, SIDE, DEPTH), jnp.float32),
        ),
        in_specs=[SMEM] * 4,
        out_specs=(VMEM, VMEM),
        compiler_params=SMALL,
        cost_estimate=pl.CostEstimate(flops=1000000, bytes_accessed=1000000, transcendentals=0),
    )(smooth, slope, band, step)


def along_matrix(matrices, axis, rows):
    return matrices[2 * axis * RIM : 2 * axis * RIM + rows, 0 : 3 * WIDE]


def depth_matrix(matrices, kind):
    return matrices[4 * RIM :, kind * DEPTH : (kind + 1) * DEPTH]


def fill_extended(extended, own, x_even, x_odd, y_even, y_odd, even_corner, odd_corner):
    extended[0:SIDE, 0:SIDE, :] = own
    gap = jnp.zeros((SLAB - REACH, WIDE, DEPTH), jnp.float32)
    columns = (slice(SIDE, SIDE + SLAB), slice(SIDE + SLAB, WIDE))
    extended[0:SIDE, columns[0], :] = y_even
    extended[0:SIDE, columns[1], :] = y_odd
    for at, part in enumerate((x_even, x_odd)):
        rows = slice(SIDE + at * SLAB, SIDE + at * SLAB + REACH)
        extended[rows, 0:SIDE, :] = part
        extended[rows.stop : SIDE + (at + 1) * SLAB, 0:WIDE, :] = gap
        extended[rows, columns[0], :] = even_corner[at * REACH : (at + 1) * REACH]
        extended[rows, columns[1], :] = odd_corner[at * REACH : (at + 1) * REACH]


def stacked_parts(value):
    high, low = split_rows(value)
    return jnp.concatenate([high, low, high], axis=0)


def lane_parts(value):
    high, low = split_rows(value)
    return jnp.concatenate([high, low, high], axis=1)


def take_place(block, place):
    outer, inner, depth = block.shape
    return block.reshape(outer * inner, depth)[pl.ds(place, outer, stride=inner), :]


def along_x_stage(extended, crossed, matrix):
    for pair in range(0, WIDE, 2):
        places = (pair, pair + 1)
        value = jnp.concatenate([take_place(extended, y) for y in places], axis=1)
        out = jnp.dot(matrix, stacked_parts(value), preferred_element_type=jnp.float32)
        for at, y in enumerate(places):
            crossed[y, 0 : out.shape[0], :] = out[:, at * DEPTH : (at + 1) * DEPTH]


def gradient_stages(extended, matrices, crossed, flat_s, flat_g, normals, lengths, finish):
    along_x_stage(extended, crossed, along_matrix(matrices, 0, 2 * RIM))
    matrix = along_matrix(matrices, 1, 2 * RIM)
    for at, row in enumerate(OUT_ROWS):
        value = jnp.concatenate(
            [take_place(crossed, row + kind * RIM) for kind in range(2)], axis=1
        )
        got = jnp.dot(matrix, stacked_parts(value), preferred_element_type=jnp.float32)
        flat_s[at, 0:RIM, :] = got[0:RIM, DEPTH:]
        flat_s[at, RIM:, :] = got[RIM:, :DEPTH]
        flat_g[at, :, :] = got[0:RIM, :DEPTH]
    weights_s = depth_matrix(matrices, 0)
    weights_g = depth_matrix(matrices, 1)
    for at in range(0, SIDE + 2, 2):
        cross = jnp.dot(
            lane_parts(flat_s[at : at + 2].reshape(4 * RIM, DEPTH)), weights_s,
            preferred_element_type=jnp.float32,
        )
        deep = jnp.dot(
            lane_parts(flat_g[at : at + 2].reshape(2 * RIM, DEPTH)), weights_g,
            preferred_element_type=jnp.float32,
        )
        for half in range(2):
            grad_x = cross[2 * half * RIM : (2 * half + 1) * RIM]
            grad_y = cross[(2 * half + 1) * RIM : (2 * half + 2) * RIM]
            grad_z = deep[half * RIM : (half + 1) * RIM]
            square = grad_x * grad_x + grad_y * grad_y + grad_z * grad_z + 1.0
            inverse = lax.rsqrt(square)
            normals[0, at + half, :, :] = grad_x * inverse
            normals[1, at + half, :, :] = grad_y * inverse
            normals[2, at + half, :, :] = grad_z * inverse
            lengths[at + half, :, :] = square * inverse
        if at > 0:
            finish(at - 2)
            finish(at - 1)


def bending(normals, x):
    lane = lax.broadcasted_iota(jnp.int32, (SIDE, DEPTH), 1)
    at = x + 1
    across = normals[1, at, :, :]
    deep = normals[2, at, 0:SIDE, :]
    bend = normals[0, at + 1, 0:SIDE, :] - normals[0, at - 1, 0:SIDE, :]
    bend += (pltpu.roll(across, RIM - 1, 0) - pltpu.roll(across, 1, 0))[0:SIDE]
    bend += jnp.where(lane < DEPTH - 1, pltpu.roll(deep, DEPTH - 1, 1), 0.0)
    bend -= jnp.where(lane > 0, pltpu.roll(deep, 1, 1), 0.0)
    return 0.25 * bend


def speed_stages(extended, matrices, crossed, flat_s, velocity, finish):
    along_x_stage(extended, crossed, along_matrix(matrices, 0, RIM + 8))
    matrix = along_matrix(matrices, 1, RIM + 8)
    for pair in range(0, len(OUT_ROWS), 2):
        value = jnp.concatenate(
            [take_place(crossed, row) for row in OUT_ROWS[pair : pair + 2]], axis=1
        )
        got = jnp.dot(matrix, stacked_parts(value), preferred_element_type=jnp.float32)
        for half in range(2):
            flat_s[pair + half, :, :] = got[0:RIM, half * DEPTH : (half + 1) * DEPTH]
    weights = depth_matrix(matrices, 0)
    for at in range(0, SIDE + 2, 2):
        got = jnp.dot(
            lane_parts(flat_s[at : at + 2].reshape(2 * RIM, DEPTH)), weights,
            preferred_element_type=jnp.float32,
        )
        velocity[at : at + 2, :, :] = got.reshape(2, RIM, DEPTH)
        if at > 0:
            finish(at - 2)
            finish(at - 1)


def face_mean(velocity, x):
    lane = lax.broadcasted_iota(jnp.int32, (SIDE, DEPTH), 1)
    at = x + 1
    rim = velocity[at, :, :]
    centre = rim[0:SIDE]
    total = centre + velocity[at + 1, 0:SIDE, :] + velocity[at - 1, 0:SIDE, :]
    total += (pltpu.roll(rim, RIM - 1, 0) + pltpu.roll(rim, 1, 0))[0:SIDE]
    total += jnp.where(lane < DEPTH - 1, pltpu.roll(centre, DEPTH - 1, 1), 0.0)
    total += jnp.where(lane > 0, pltpu.roll(centre, 1, 1), 0.0)
    return total / 7.0


HALOS = 5


def stacked_halos(halos, part):
    x_even, x_odd, y_odd = [halo[part] for halo in halos[:3]]
    even_slab, odd_corner = [halo[...] for halo in halos[3:]]
    return x_even, x_odd, even_slab[0:SIDE], y_odd, even_slab[SIDE:], odd_corner


def bend_kernel(own, *refs):
    halos = refs[:HALOS]
    matrices, gain, base, push = refs[HALOS : HALOS + 4]
    extended, crossed, flat_s, flat_g, normals, lengths = refs[HALOS + 4 :]
    fill_extended(extended, own[...], *stacked_halos(halos, 1))

    def finish(x):
        factor = gain[x // (SIDE // 2), :, :] * lengths[x + 1, 0:SIDE, :]
        push[x, :, :] = factor
        base[x, :, :] = own[x, :, :] + factor * bending(normals, x)

    gradient_stages(extended, matrices, crossed, flat_s, flat_g, normals, lengths, finish)


def speed_kernel(own, *refs):
    halos = refs[:HALOS]
    matrices, base, push, out, speed = refs[HALOS : HALOS + 5]
    extended, crossed, flat_s, velocity = refs[HALOS + 5 :]
    fill_extended(extended, own[...], *stacked_halos(halos, 0))

    def finish(x):
        value = face_mean(velocity, x)
        speed[x, :, :] = value
        out[x, :, :] = base[x, :, :] - push[x, :, :] * value

    speed_stages(extended, matrices, crossed, flat_s, velocity, finish)


def later_kernel(own, *refs):
    halos = refs[: HALOS + 1]
    matrices, gain, speed, out = refs[HALOS + 1 : HALOS + 5]
    extended, crossed, flat_s, flat_g, normals, lengths = refs[HALOS + 5 :]
    fill_extended(extended, own[...], *[halo[...] for halo in halos])

    def finish(x):
        factor = gain[x // (SIDE // 2), :, :] * lengths[x + 1, 0:SIDE, :]
        out[x, :, :] = own[x, :, :] - factor * (speed[x, :, :] - bending(normals, x))

    gradient_stages(extended, matrices, crossed, flat_s, flat_g, normals, lengths, finish)


def call_kernel(body, arrays, outputs, scratch):
    shape = jax.ShapeDtypeStruct((SIDE, SIDE, DEPTH), jnp.float32)
    return pl.pallas_call(
        body,
        out_shape=(shape,) * outputs,
        in_specs=[VMEM] * len(arrays),
        out_specs=(VMEM,) * outputs,
        scratch_shapes=[pltpu.VMEM(shape, jnp.float32) for shape in scratch],
        compiler_params=pltpu.CompilerParams(vmem_limit_bytes=20 * 1024 * 1024),
    )(*arrays)


def corner_kernel(part, own, x_even, x_odd, even, odd):
    parity = lax.axis_index("gy") & 1
    starts = [
        pl.multiple_of(jnp.where(parity == side, SIDE - SLAB, 0), SLAB) for side in range(2)
    ]
    offset = even.shape[0] - 2 * REACH
    if offset:
        even[0:SIDE, :, :] = own[:, pl.ds(starts[0], SLAB), :]
    for at, x_halo in enumerate((x_even, x_odd)):
        source = x_halo if part is None else x_halo.at[part]
        rows = slice(at * REACH, (at + 1) * REACH)
        even[offset + rows.start : offset + rows.stop, :, :] = source[:, pl.ds(starts[0], SLAB), :]
        odd[rows, :, :] = source[:, pl.ds(starts[1], SLAB), :]


def corner_sides(own, x_halos, part=None):
    offset = 0 if part is None else SIDE
    return pl.pallas_call(
        functools.partial(corner_kernel, part),
        out_shape=(
            jax.ShapeDtypeStruct((offset + 2 * REACH, SLAB, DEPTH), jnp.float32),
            jax.ShapeDtypeStruct((2 * REACH, SLAB, DEPTH), jnp.float32),
        ),
        in_specs=[VMEM] * 3,
        out_specs=(VMEM, VMEM),
        compiler_params=SMALL,
    )(own, *x_halos)


def copy_kernel(source, target):
    target[...] = source[...]


def settle(block):
    return pl.pallas_call(
        copy_kernel,
        out_shape=jax.ShapeDtypeStruct(block.shape, block.dtype),
        in_specs=[VMEM],
        out_specs=VMEM,
        compiler_params=SMALL,
    )(block)


def swap(block, axis, first):
    pairs = []
    for low in range(first, lax.axis_size(axis) - 1, 2):
        pairs += [(low, low + 1), (low + 1, low)]
    return lax.ppermute(block, axis, pairs)


def both_sides(block, dim, width, parity):
    length = block.shape[dim]
    high = jnp.where(parity == 0, length - width, 0)
    return (
        lax.dynamic_slice_in_dim(block, high, width, dim),
        lax.dynamic_slice_in_dim(block, length - width - high, width, dim),
    )


def stack_kernel(*refs):
    count = (len(refs) - 2) // 2
    for at in range(count):
        for side in range(2):
            refs[2 * count + side][at] = refs[2 * at + side][...]


def stacked_sides(blocks, dim, width, parity):
    pieces = [piece for block in blocks for piece in both_sides(block, dim, width, parity)]
    out = jax.ShapeDtypeStruct((len(blocks), *pieces[0].shape), jnp.float32)
    return pl.pallas_call(
        stack_kernel,
        out_shape=(out, out),
        in_specs=[VMEM] * len(pieces),
        out_specs=(VMEM, VMEM),
        compiler_params=SMALL,
    )(*pieces)


def swap_sides(pieces, axis):
    odd = swap(pieces[1], axis, 1)
    even = swap(pieces[0], axis, 0)
    return even, odd


def per_device(level_set, sensitivity, smooth_taps, slope_taps, band, time_step):
    parity = [lax.axis_index(axis) & 1 for axis in ("gx", "gy")]
    fields = [sensitivity, level_set]
    x_halos = swap_sides(stacked_sides(fields, 0, REACH, parity[0]), "gx")
    y_odd = swap(jnp.stack([both_sides(f, 1, SLAB, parity[1])[1] for f in fields]), "gy", 1)
    matrices = prepare(smooth_taps, slope_taps, band, time_step)
    x_halos = (x_halos[0], settle(x_halos[1]))
    x_halos, matrices = lax.optimization_barrier((x_halos, matrices))
    matrices, gain = matrices
    corners = swap_sides(corner_sides(level_set, x_halos, 1), "gy")
    corners_s = swap_sides(corner_sides(sensitivity, x_halos, 0), "gy")
    rim = SIDE + 2
    gradient_scratch = [
        (WIDE, WIDE + 8, DEPTH), (WIDE, 2 * RIM + 8, DEPTH), (rim, 2 * RIM, DEPTH),
        (rim, RIM, DEPTH), (3, rim, RIM, DEPTH), (rim, RIM, DEPTH),
    ]
    speed_scratch = [
        (WIDE, WIDE + 8, DEPTH), (WIDE, RIM + 16, DEPTH), (rim, RIM, DEPTH), (rim, RIM, DEPTH)
    ]
    base, push = call_kernel(
        bend_kernel, (level_set, *x_halos, y_odd, *corners, matrices, gain), 2, gradient_scratch
    )
    phi, speed = call_kernel(
        speed_kernel, (sensitivity, *x_halos, y_odd, *corners_s, matrices, base, push), 2,
        speed_scratch,
    )
    for _ in range(1, UPDATES):
        x_halos = swap_sides(both_sides(phi, 0, REACH, parity[0]), "gx")
        y_halos = swap_sides(both_sides(phi, 1, SLAB, parity[1]), "gy")
        corners = swap_sides(corner_sides(phi, x_halos), "gy")
        (phi,) = call_kernel(
            later_kernel, (phi, *x_halos, *y_halos, *corners, matrices, gain, speed), 1, gradient_scratch,
        )
    return phi


def solution(mesh):
    return jax.shard_map(
        per_device,
        mesh=mesh,
        in_specs=(P("gx", "gy", None), P("gx", "gy", None), P(), P(), P("gx", "gy", None), P()),
        out_specs=P("gx", "gy", None),
        check_vma=False,
    )
```

```python
import jax
import jax.numpy as jnp
from jax import lax
from jax.experimental import pallas as pl
from jax.experimental.pallas import tpu as pltpu
from jax.sharding import PartitionSpec as P

UPDATES = 2
REACH = 13
SLAB = 16
SIDE = 32
RIM = 40
WIDE = 64
DEPTH = 128
TAPS = 25

OUT_ROWS = [RIM - 1] + list(range(SIDE + 1))


def split_rows(value):
    high = value.astype(jnp.bfloat16)
    low = (value - high.astype(jnp.float32)).astype(jnp.bfloat16)
    return high, low


def tap_select(index, taps):
    total = jnp.zeros(index.shape, jnp.float32)
    for k in range(TAPS):
        total = jnp.where(index == k, taps[k], total)
    return total


def side_matrix(axis, smooth, slope):
    at = lax.axis_index(axis)
    last = lax.axis_size(axis) - 1
    shape = (RIM, 3 * WIDE)
    row = lax.broadcasted_iota(jnp.int32, shape, 0)
    column = lax.broadcasted_iota(jnp.int32, shape, 1)
    place = column & (WIDE - 1)
    width = REACH if axis == "gx" else SLAB
    source = place
    for slot, side in ((0, at & 1), (1, 1 - (at & 1))):
        start = SIDE + slot * SLAB
        moved = place - start + jnp.where(side == 0, SIDE, -width)
        source = jnp.where((place >= start) & (place < start + SLAB), moved, source)
        source = jnp.where((place >= start + width) & (place < start + SLAB), -WIDE, source)
    target = jnp.where(row < RIM - 1, row, -1)
    index = source - target + TAPS // 2
    inside = (row < SIDE) | ((row == SIDE) & (at < last)) | ((row == RIM - 1) & (at > 0))
    index = jnp.where(inside, index, -1)
    parts = []
    for taps in (smooth, slope):
        full = tap_select(index, taps)
        high = full.astype(jnp.bfloat16).astype(jnp.float32)
        parts.append(jnp.where(column < 2 * WIDE, high, full - high))
    return jnp.concatenate(parts, axis=0).astype(jnp.bfloat16)


def block_gain(band, step, p):
    blocks_y, blocks_z = 2, 4
    rows = SIDE // blocks_y
    lane = lax.broadcasted_iota(jnp.int32, (rows, DEPTH), 1) // (DEPTH // blocks_z)
    parts = []
    for q in range(blocks_y):
        value = jnp.zeros(lane.shape, jnp.float32)
        for r in range(blocks_z):
            entry = band[p, q, r].astype(jnp.float32) * step[0]
            value = jnp.where(lane == r, entry, value)
        parts.append(value)
    return jnp.concatenate(parts, axis=0)


def prepare_kernel(smooth, slope, band, step, out, gain):
    for p in range(2):
        gain[p, :, :] = block_gain(band, step, p)
    for at, axis in enumerate(("gx", "gy")):
        out[2 * at * RIM : 2 * (at + 1) * RIM, 0 : 3 * WIDE] = side_matrix(axis, smooth, slope)
        out[2 * at * RIM : 2 * (at + 1) * RIM, 3 * WIDE :] = jnp.zeros((2 * RIM, WIDE), jnp.bfloat16)
    shape = (DEPTH, DEPTH)
    index = (
        lax.broadcasted_iota(jnp.int32, shape, 0)
        - lax.broadcasted_iota(jnp.int32, shape, 1)
        + TAPS // 2
    )
    for at, taps in enumerate((smooth, slope)):
        columns = slice(at * DEPTH, (at + 1) * DEPTH)
        high, low = split_rows(tap_select(index, taps))
        out[4 * RIM : 4 * RIM + DEPTH, columns] = high
        out[4 * RIM + DEPTH : 4 * RIM + 2 * DEPTH, columns] = high
        out[4 * RIM + 2 * DEPTH :, columns] = low


SMEM = pl.BlockSpec(memory_space=pltpu.SMEM)
VMEM = pl.BlockSpec(memory_space=pltpu.VMEM)
SMALL = pltpu.CompilerParams(vmem_limit_bytes=4 * 1024 * 1024)


def prepare(smooth, slope, band, step):
    return pl.pallas_call(
        prepare_kernel,
        out_shape=(
            jax.ShapeDtypeStruct((4 * RIM + 3 * DEPTH, 2 * DEPTH), jnp.bfloat16),
            jax.ShapeDtypeStruct((2, SIDE, DEPTH), jnp.float32),
        ),
        in_specs=[SMEM] * 4,
        out_specs=(VMEM, VMEM),
        compiler_params=SMALL,
        cost_estimate=pl.CostEstimate(flops=1000000, bytes_accessed=1000000, transcendentals=0),
    )(smooth, slope, band, step)


def along_matrix(matrices, axis, rows):
    return matrices[2 * axis * RIM : 2 * axis * RIM + rows, 0 : 3 * WIDE]


def depth_matrix(matrices, kind):
    return matrices[4 * RIM :, kind * DEPTH : (kind + 1) * DEPTH]


def fill_extended(extended, own, x_even, x_odd, y_even, y_odd, even_corner, odd_corner):
    extended[0:SIDE, 0:SIDE, :] = own
    gap = jnp.zeros((SLAB - REACH, WIDE, DEPTH), jnp.float32)
    columns = (slice(SIDE, SIDE + SLAB), slice(SIDE + SLAB, WIDE))
    extended[0:SIDE, columns[0], :] = y_even
    extended[0:SIDE, columns[1], :] = y_odd
    for at, part in enumerate((x_even, x_odd)):
        rows = slice(SIDE + at * SLAB, SIDE + at * SLAB + REACH)
        extended[rows, 0:SIDE, :] = part
        extended[rows.stop : SIDE + (at + 1) * SLAB, 0:WIDE, :] = gap
        extended[rows, columns[0], :] = even_corner[at * REACH : (at + 1) * REACH]
        extended[rows, columns[1], :] = odd_corner[at * REACH : (at + 1) * REACH]


def stacked_parts(value):
    high, low = split_rows(value)
    return jnp.concatenate([high, low, high], axis=0)


def lane_parts(value):
    high, low = split_rows(value)
    return jnp.concatenate([high, low, high], axis=1)


def take_place(block, place):
    outer, inner, depth = block.shape
    return block.reshape(outer * inner, depth)[pl.ds(place, outer, stride=inner), :]


def along_x_stage(extended, crossed, matrix):
    for pair in range(0, WIDE, 2):
        places = (pair, pair + 1)
        value = jnp.concatenate([take_place(extended, y) for y in places], axis=1)
        out = jnp.dot(matrix, stacked_parts(value), preferred_element_type=jnp.float32)
        for at, y in enumerate(places):
            crossed[y, 0 : out.shape[0], :] = out[:, at * DEPTH : (at + 1) * DEPTH]


def gradient_stages(extended, matrices, crossed, flat_s, flat_g, normals, lengths, finish):
    along_x_stage(extended, crossed, along_matrix(matrices, 0, 2 * RIM))
    matrix = along_matrix(matrices, 1, 2 * RIM)
    for at, row in enumerate(OUT_ROWS):
        value = jnp.concatenate(
            [take_place(crossed, row + kind * RIM) for kind in range(2)], axis=1
        )
        got = jnp.dot(matrix, stacked_parts(value), preferred_element_type=jnp.float32)
        flat_s[at, 0:RIM, :] = got[0:RIM, DEPTH:]
        flat_s[at, RIM:, :] = got[RIM:, :DEPTH]
        flat_g[at, :, :] = got[0:RIM, :DEPTH]
    weights_s = depth_matrix(matrices, 0)
    weights_g = depth_matrix(matrices, 1)
    for at in range(0, SIDE + 2, 2):
        cross = jnp.dot(
            lane_parts(flat_s[at : at + 2].reshape(4 * RIM, DEPTH)), weights_s,
            preferred_element_type=jnp.float32,
        )
        deep = jnp.dot(
            lane_parts(flat_g[at : at + 2].reshape(2 * RIM, DEPTH)), weights_g,
            preferred_element_type=jnp.float32,
        )
        for half in range(2):
            grad_x = cross[2 * half * RIM : (2 * half + 1) * RIM]
            grad_y = cross[(2 * half + 1) * RIM : (2 * half + 2) * RIM]
            grad_z = deep[half * RIM : (half + 1) * RIM]
            square = grad_x * grad_x + grad_y * grad_y + grad_z * grad_z + 1.0
            inverse = lax.rsqrt(square)
            normals[0, at + half, :, :] = grad_x * inverse
            normals[1, at + half, :, :] = grad_y * inverse
            normals[2, at + half, :, :] = grad_z * inverse
            lengths[at + half, :, :] = square * inverse
        if at > 0:
            finish(at - 2)
            finish(at - 1)


def bending(normals, x):
    lane = lax.broadcasted_iota(jnp.int32, (SIDE, DEPTH), 1)
    at = x + 1
    across = normals[1, at, :, :]
    deep = normals[2, at, 0:SIDE, :]
    bend = normals[0, at + 1, 0:SIDE, :] - normals[0, at - 1, 0:SIDE, :]
    bend += (pltpu.roll(across, RIM - 1, 0) - pltpu.roll(across, 1, 0))[0:SIDE]
    bend += jnp.where(lane < DEPTH - 1, pltpu.roll(deep, DEPTH - 1, 1), 0.0)
    bend -= jnp.where(lane > 0, pltpu.roll(deep, 1, 1), 0.0)
    return 0.25 * bend


def speed_stages(extended, matrices, crossed, flat_s, velocity, finish):
    along_x_stage(extended, crossed, along_matrix(matrices, 0, RIM + 8))
    matrix = along_matrix(matrices, 1, RIM + 8)
    for pair in range(0, len(OUT_ROWS), 2):
        value = jnp.concatenate(
            [take_place(crossed, row) for row in OUT_ROWS[pair : pair + 2]], axis=1
        )
        got = jnp.dot(matrix, stacked_parts(value), preferred_element_type=jnp.float32)
        for half in range(2):
            flat_s[pair + half, :, :] = got[0:RIM, half * DEPTH : (half + 1) * DEPTH]
    weights = depth_matrix(matrices, 0)
    for at in range(0, SIDE + 2, 2):
        got = jnp.dot(
            lane_parts(flat_s[at : at + 2].reshape(2 * RIM, DEPTH)), weights,
            preferred_element_type=jnp.float32,
        )
        velocity[at : at + 2, :, :] = got.reshape(2, RIM, DEPTH)
        if at > 0:
            finish(at - 2)
            finish(at - 1)


def face_mean(velocity, x):
    lane = lax.broadcasted_iota(jnp.int32, (SIDE, DEPTH), 1)
    at = x + 1
    rim = velocity[at, :, :]
    centre = rim[0:SIDE]
    total = centre + velocity[at + 1, 0:SIDE, :] + velocity[at - 1, 0:SIDE, :]
    total += (pltpu.roll(rim, RIM - 1, 0) + pltpu.roll(rim, 1, 0))[0:SIDE]
    total += jnp.where(lane < DEPTH - 1, pltpu.roll(centre, DEPTH - 1, 1), 0.0)
    total += jnp.where(lane > 0, pltpu.roll(centre, 1, 1), 0.0)
    return total / 7.0


HALOS = 5


def stacked_halos(halos, part):
    x_even, x_odd, even_slab, odd_corner = [halos[at][...] for at in (0, 1, 3, 4)]
    return x_even, x_odd, even_slab[0:SIDE], halos[2][part], even_slab[SIDE:], odd_corner


def bend_kernel(own, *refs):
    halos = refs[:HALOS]
    matrices, gain, base, push = refs[HALOS : HALOS + 4]
    extended, crossed, flat_s, flat_g, normals, lengths = refs[HALOS + 4 :]
    fill_extended(extended, own[...], *stacked_halos(halos, 1))

    def finish(x):
        factor = gain[x // (SIDE // 2), :, :] * lengths[x + 1, 0:SIDE, :]
        push[x, :, :] = factor
        base[x, :, :] = own[x, :, :] + factor * bending(normals, x)

    gradient_stages(extended, matrices, crossed, flat_s, flat_g, normals, lengths, finish)


def speed_kernel(own, *refs):
    halos = refs[:HALOS]
    matrices, base, push, out, speed = refs[HALOS : HALOS + 5]
    extended, crossed, flat_s, velocity = refs[HALOS + 5 :]
    fill_extended(extended, own[...], *stacked_halos(halos, 0))

    def finish(x):
        value = face_mean(velocity, x)
        speed[x, :, :] = value
        out[x, :, :] = base[x, :, :] - push[x, :, :] * value

    speed_stages(extended, matrices, crossed, flat_s, velocity, finish)


def later_kernel(own, *refs):
    halos = refs[: HALOS + 1]
    matrices, gain, speed, out = refs[HALOS + 1 : HALOS + 5]
    extended, crossed, flat_s, flat_g, normals, lengths = refs[HALOS + 5 :]
    fill_extended(extended, own[...], *[halo[...] for halo in halos])

    def finish(x):
        factor = gain[x // (SIDE // 2), :, :] * lengths[x + 1, 0:SIDE, :]
        out[x, :, :] = own[x, :, :] - factor * (speed[x, :, :] - bending(normals, x))

    gradient_stages(extended, matrices, crossed, flat_s, flat_g, normals, lengths, finish)


def call_kernel(body, arrays, outputs, scratch):
    shape = jax.ShapeDtypeStruct((SIDE, SIDE, DEPTH), jnp.float32)
    return pl.pallas_call(
        body,
        out_shape=(shape,) * outputs,
        in_specs=[VMEM] * len(arrays),
        out_specs=(VMEM,) * outputs,
        scratch_shapes=[pltpu.VMEM(shape, jnp.float32) for shape in scratch],
        compiler_params=pltpu.CompilerParams(vmem_limit_bytes=20 * 1024 * 1024),
    )(*arrays)


def corner_kernel(own, x_even, x_odd, even, odd):
    parity = lax.axis_index("gy") & 1
    starts = [
        pl.multiple_of(jnp.where(parity == side, SIDE - SLAB, 0), SLAB) for side in range(2)
    ]
    offset = even.shape[0] - 2 * REACH
    if offset:
        even[0:SIDE, :, :] = own[:, pl.ds(starts[0], SLAB), :]
    for at, source in enumerate((x_even, x_odd)):
        rows = slice(at * REACH, (at + 1) * REACH)
        even[offset + rows.start : offset + rows.stop, :, :] = source[:, pl.ds(starts[0], SLAB), :]
        odd[rows, :, :] = source[:, pl.ds(starts[1], SLAB), :]


def corner_sides(own, x_halos, offset=0):
    return pl.pallas_call(
        corner_kernel,
        out_shape=(
            jax.ShapeDtypeStruct((offset + 2 * REACH, SLAB, DEPTH), jnp.float32),
            jax.ShapeDtypeStruct((2 * REACH, SLAB, DEPTH), jnp.float32),
        ),
        in_specs=[VMEM] * 3,
        out_specs=(VMEM, VMEM),
        compiler_params=SMALL,
    )(own, *x_halos)


def copy_kernel(source, target):
    target[...] = source[...]


def settle(block):
    return pl.pallas_call(
        copy_kernel,
        out_shape=jax.ShapeDtypeStruct(block.shape, block.dtype),
        in_specs=[VMEM],
        out_specs=VMEM,
        compiler_params=SMALL,
    )(block)


def swap(block, axis, first):
    pairs = []
    for low in range(first, lax.axis_size(axis) - 1, 2):
        pairs += [(low, low + 1), (low + 1, low)]
    return lax.ppermute(block, axis, pairs)


def both_sides(block, dim, width, parity):
    length = block.shape[dim]
    high = jnp.where(parity == 0, length - width, 0)
    return (
        lax.dynamic_slice_in_dim(block, high, width, dim),
        lax.dynamic_slice_in_dim(block, length - width - high, width, dim),
    )


def swap_sides(pieces, axis):
    odd = swap(pieces[1], axis, 1)
    even = swap(pieces[0], axis, 0)
    return even, odd


def per_device(level_set, sensitivity, smooth_taps, slope_taps, band, time_step):
    parity = [lax.axis_index(axis) & 1 for axis in ("gx", "gy")]
    fields = [sensitivity, level_set]
    x_halos = swap_sides(both_sides(level_set, 0, REACH, parity[0]), "gx")
    x_halos_s = swap_sides(both_sides(sensitivity, 0, REACH, parity[0]), "gx")
    y_odd = swap(jnp.stack([both_sides(f, 1, SLAB, parity[1])[1] for f in fields]), "gy", 1)
    matrices = prepare(smooth_taps, slope_taps, band, time_step)
    x_halos = (x_halos[0], settle(x_halos[1]))
    matrices, gain = matrices
    pieces = corner_sides(level_set, x_halos, SIDE)
    corners = swap_sides(pieces, "gy")
    x_odd, matrices, gain = lax.optimization_barrier((x_halos_s[1], matrices, gain))
    x_halos_s = (x_halos_s[0], settle(x_odd))
    corners_s = swap_sides(corner_sides(sensitivity, x_halos_s, SIDE), "gy")
    rim = SIDE + 2
    gradient_scratch = [
        (WIDE, WIDE + 8, DEPTH), (WIDE, 2 * RIM + 8, DEPTH), (rim, 2 * RIM, DEPTH),
        (rim, RIM, DEPTH), (3, rim, RIM, DEPTH), (rim, RIM, DEPTH),
    ]
    speed_scratch = [
        (WIDE, WIDE + 8, DEPTH), (WIDE, RIM + 16, DEPTH), (rim, RIM, DEPTH), (rim, RIM, DEPTH)
    ]
    base, push = call_kernel(
        bend_kernel, (level_set, *x_halos, y_odd, *corners, matrices, gain), 2, gradient_scratch
    )
    phi, speed = call_kernel(
        speed_kernel, (sensitivity, *x_halos_s, y_odd, *corners_s, matrices, base, push), 2,
        speed_scratch,
    )
    for _ in range(1, UPDATES):
        x_halos = swap_sides(both_sides(phi, 0, REACH, parity[0]), "gx")
        y_halos = swap_sides(both_sides(phi, 1, SLAB, parity[1]), "gy")
        corners = swap_sides(corner_sides(phi, x_halos), "gy")
        (phi,) = call_kernel(
            later_kernel, (phi, *x_halos, *y_halos, *corners, matrices, gain, speed), 1, gradient_scratch,
        )
    return phi


def solution(mesh):
    return jax.shard_map(
        per_device,
        mesh=mesh,
        in_specs=(P("gx", "gy", None), P("gx", "gy", None), P(), P(), P("gx", "gy", None), P()),
        out_specs=P("gx", "gy", None),
        check_vma=False,
    )
```

```python
import jax
import jax.numpy as jnp
from jax import lax
from jax.experimental import pallas as pl
from jax.experimental.pallas import tpu as pltpu
from jax.sharding import PartitionSpec as P

UPDATES = 2
REACH = 13
SLAB = 16
SIDE = 32
RIM = 40
WIDE = 64
DEPTH = 128
TAPS = 25

OUT_ROWS = [RIM - 1] + list(range(SIDE + 1))


def split_rows(value):
    high = value.astype(jnp.bfloat16)
    low = (value - high.astype(jnp.float32)).astype(jnp.bfloat16)
    return high, low


def tap_select(index, taps):
    total = jnp.zeros(index.shape, jnp.float32)
    for k in range(TAPS):
        total = jnp.where(index == k, taps[k], total)
    return total


def side_matrix(axis, smooth, slope):
    at = lax.axis_index(axis)
    last = lax.axis_size(axis) - 1
    shape = (RIM, 3 * WIDE)
    row = lax.broadcasted_iota(jnp.int32, shape, 0)
    column = lax.broadcasted_iota(jnp.int32, shape, 1)
    place = column & (WIDE - 1)
    width = REACH if axis == "gx" else SLAB
    source = place
    for slot, side in ((0, at & 1), (1, 1 - (at & 1))):
        start = SIDE + slot * SLAB
        moved = place - start + jnp.where(side == 0, SIDE, -width)
        source = jnp.where((place >= start) & (place < start + SLAB), moved, source)
        source = jnp.where((place >= start + width) & (place < start + SLAB), -WIDE, source)
    target = jnp.where(row < RIM - 1, row, -1)
    index = source - target + TAPS // 2
    inside = (row < SIDE) | ((row == SIDE) & (at < last)) | ((row == RIM - 1) & (at > 0))
    index = jnp.where(inside, index, -1)
    parts = []
    for taps in (smooth, slope):
        full = tap_select(index, taps)
        high = full.astype(jnp.bfloat16).astype(jnp.float32)
        parts.append(jnp.where(column < 2 * WIDE, high, full - high))
    return jnp.concatenate(parts, axis=0).astype(jnp.bfloat16)


def block_gain(band, step, p):
    blocks_y, blocks_z = 2, 4
    rows = SIDE // blocks_y
    lane = lax.broadcasted_iota(jnp.int32, (rows, DEPTH), 1) // (DEPTH // blocks_z)
    parts = []
    for q in range(blocks_y):
        value = jnp.zeros(lane.shape, jnp.float32)
        for r in range(blocks_z):
            entry = band[p, q, r].astype(jnp.float32) * step[0]
            value = jnp.where(lane == r, entry, value)
        parts.append(value)
    return jnp.concatenate(parts, axis=0)


def prepare_kernel(smooth, slope, band, step, out, gain):
    for p in range(2):
        gain[p, :, :] = block_gain(band, step, p)
    for at, axis in enumerate(("gx", "gy")):
        out[2 * at * RIM : 2 * (at + 1) * RIM, 0 : 3 * WIDE] = side_matrix(axis, smooth, slope)
        out[2 * at * RIM : 2 * (at + 1) * RIM, 3 * WIDE :] = jnp.zeros((2 * RIM, WIDE), jnp.bfloat16)
    shape = (DEPTH, DEPTH)
    index = (
        lax.broadcasted_iota(jnp.int32, shape, 0)
        - lax.broadcasted_iota(jnp.int32, shape, 1)
        + TAPS // 2
    )
    for at, taps in enumerate((smooth, slope)):
        columns = slice(at * DEPTH, (at + 1) * DEPTH)
        high, low = split_rows(tap_select(index, taps))
        out[4 * RIM : 4 * RIM + DEPTH, columns] = high
        out[4 * RIM + DEPTH : 4 * RIM + 2 * DEPTH, columns] = high
        out[4 * RIM + 2 * DEPTH :, columns] = low


SMEM = pl.BlockSpec(memory_space=pltpu.SMEM)
VMEM = pl.BlockSpec(memory_space=pltpu.VMEM)
SMALL = pltpu.CompilerParams(vmem_limit_bytes=4 * 1024 * 1024)


def prepare(smooth, slope, band, step):
    return pl.pallas_call(
        prepare_kernel,
        out_shape=(
            jax.ShapeDtypeStruct((4 * RIM + 3 * DEPTH, 2 * DEPTH), jnp.bfloat16),
            jax.ShapeDtypeStruct((2, SIDE, DEPTH), jnp.float32),
        ),
        in_specs=[SMEM] * 4,
        out_specs=(VMEM, VMEM),
        compiler_params=SMALL,
        cost_estimate=pl.CostEstimate(flops=1000000, bytes_accessed=1000000, transcendentals=0),
    )(smooth, slope, band, step)


def along_matrix(matrices, axis, rows):
    return matrices[2 * axis * RIM : 2 * axis * RIM + rows, 0 : 3 * WIDE]


def depth_matrix(matrices, kind):
    return matrices[4 * RIM :, kind * DEPTH : (kind + 1) * DEPTH]


def fill_extended(extended, own, x_even, x_odd, y_even, y_odd, even_corner, odd_corner):
    extended[0:SIDE, 0:SIDE, :] = own
    gap = jnp.zeros((SLAB - REACH, WIDE, DEPTH), jnp.float32)
    columns = (slice(SIDE, SIDE + SLAB), slice(SIDE + SLAB, WIDE))
    extended[0:SIDE, columns[0], :] = y_even
    extended[0:SIDE, columns[1], :] = y_odd
    for at, part in enumerate((x_even, x_odd)):
        rows = slice(SIDE + at * SLAB, SIDE + at * SLAB + REACH)
        extended[rows, 0:SIDE, :] = part
        extended[rows.stop : SIDE + (at + 1) * SLAB, 0:WIDE, :] = gap
        extended[rows, columns[0], :] = even_corner[at * REACH : (at + 1) * REACH]
        extended[rows, columns[1], :] = odd_corner[at * REACH : (at + 1) * REACH]


def stacked_parts(value):
    high, low = split_rows(value)
    return jnp.concatenate([high, low, high], axis=0)


def lane_parts(value):
    high, low = split_rows(value)
    return jnp.concatenate([high, low, high], axis=1)


def take_place(block, place):
    outer, inner, depth = block.shape
    return block.reshape(outer * inner, depth)[pl.ds(place, outer, stride=inner), :]


def along_x_stage(extended, crossed, matrix):
    for pair in range(0, WIDE, 2):
        places = (pair, pair + 1)
        value = jnp.concatenate([take_place(extended, y) for y in places], axis=1)
        out = jnp.dot(matrix, stacked_parts(value), preferred_element_type=jnp.float32)
        for at, y in enumerate(places):
            crossed[y, 0 : out.shape[0], :] = out[:, at * DEPTH : (at + 1) * DEPTH]


def gradient_stages(extended, matrices, crossed, flat_s, flat_g, normals, lengths, finish):
    along_x_stage(extended, crossed, along_matrix(matrices, 0, 2 * RIM))
    matrix = along_matrix(matrices, 1, 2 * RIM)
    for at, row in enumerate(OUT_ROWS):
        value = jnp.concatenate(
            [take_place(crossed, row + kind * RIM) for kind in range(2)], axis=1
        )
        got = jnp.dot(matrix, stacked_parts(value), preferred_element_type=jnp.float32)
        flat_s[at, 0:RIM, :] = got[0:RIM, DEPTH:]
        flat_s[at, RIM:, :] = got[RIM:, :DEPTH]
        flat_g[at, :, :] = got[0:RIM, :DEPTH]
    weights_s = depth_matrix(matrices, 0)
    weights_g = depth_matrix(matrices, 1)
    for at in range(0, SIDE + 2, 2):
        cross = jnp.dot(
            lane_parts(flat_s[at : at + 2].reshape(4 * RIM, DEPTH)), weights_s,
            preferred_element_type=jnp.float32,
        )
        deep = jnp.dot(
            lane_parts(flat_g[at : at + 2].reshape(2 * RIM, DEPTH)), weights_g,
            preferred_element_type=jnp.float32,
        )
        for half in range(2):
            grad_x = cross[2 * half * RIM : (2 * half + 1) * RIM]
            grad_y = cross[(2 * half + 1) * RIM : (2 * half + 2) * RIM]
            grad_z = deep[half * RIM : (half + 1) * RIM]
            square = grad_x * grad_x + grad_y * grad_y + grad_z * grad_z + 1.0
            inverse = lax.rsqrt(square)
            normals[0, at + half, :, :] = grad_x * inverse
            normals[1, at + half, :, :] = grad_y * inverse
            normals[2, at + half, :, :] = grad_z * inverse
            lengths[at + half, :, :] = square * inverse
        if at > 0:
            finish(at - 2)
            finish(at - 1)


def bending(normals, x):
    lane = lax.broadcasted_iota(jnp.int32, (SIDE, DEPTH), 1)
    at = x + 1
    across = normals[1, at, :, :]
    deep = normals[2, at, 0:SIDE, :]
    bend = normals[0, at + 1, 0:SIDE, :] - normals[0, at - 1, 0:SIDE, :]
    bend += (pltpu.roll(across, RIM - 1, 0) - pltpu.roll(across, 1, 0))[0:SIDE]
    bend += jnp.where(lane < DEPTH - 1, pltpu.roll(deep, DEPTH - 1, 1), 0.0)
    bend -= jnp.where(lane > 0, pltpu.roll(deep, 1, 1), 0.0)
    return 0.25 * bend


def speed_stages(extended, matrices, crossed, flat_s, velocity, finish):
    along_x_stage(extended, crossed, along_matrix(matrices, 0, RIM + 8))
    matrix = along_matrix(matrices, 1, RIM + 8)
    for pair in range(0, len(OUT_ROWS), 2):
        value = jnp.concatenate(
            [take_place(crossed, row) for row in OUT_ROWS[pair : pair + 2]], axis=1
        )
        got = jnp.dot(matrix, stacked_parts(value), preferred_element_type=jnp.float32)
        for half in range(2):
            flat_s[pair + half, :, :] = got[0:RIM, half * DEPTH : (half + 1) * DEPTH]
    weights = depth_matrix(matrices, 0)
    for at in range(0, SIDE + 2, 2):
        got = jnp.dot(
            lane_parts(flat_s[at : at + 2].reshape(2 * RIM, DEPTH)), weights,
            preferred_element_type=jnp.float32,
        )
        velocity[at : at + 2, :, :] = got.reshape(2, RIM, DEPTH)
        if at > 0:
            finish(at - 2)
            finish(at - 1)


def face_mean(velocity, x):
    lane = lax.broadcasted_iota(jnp.int32, (SIDE, DEPTH), 1)
    at = x + 1
    rim = velocity[at, :, :]
    centre = rim[0:SIDE]
    total = centre + velocity[at + 1, 0:SIDE, :] + velocity[at - 1, 0:SIDE, :]
    total += (pltpu.roll(rim, RIM - 1, 0) + pltpu.roll(rim, 1, 0))[0:SIDE]
    total += jnp.where(lane < DEPTH - 1, pltpu.roll(centre, DEPTH - 1, 1), 0.0)
    total += jnp.where(lane > 0, pltpu.roll(centre, 1, 1), 0.0)
    return total * (1.0 / 7.0)


HALOS = 5


def stacked_halos(halos, part):
    x_even, x_odd, even_slab, odd_corner = [halos[at][...] for at in (0, 1, 3, 4)]
    return x_even, x_odd, even_slab[0:SIDE], halos[2][part], even_slab[SIDE:], odd_corner


def bend_kernel(own, *refs):
    halos = refs[:HALOS]
    matrices, gain, base, push = refs[HALOS : HALOS + 4]
    extended, crossed, flat_s, flat_g, normals, lengths = refs[HALOS + 4 :]
    fill_extended(extended, own[...], *stacked_halos(halos, 1))

    def finish(x):
        factor = gain[x // (SIDE // 2), :, :] * lengths[x + 1, 0:SIDE, :]
        push[x, :, :] = factor
        base[x, :, :] = own[x, :, :] + factor * bending(normals, x)

    gradient_stages(extended, matrices, crossed, flat_s, flat_g, normals, lengths, finish)


def speed_kernel(own, *refs):
    halos = refs[:HALOS]
    matrices, base, push, out, speed = refs[HALOS : HALOS + 5]
    extended, crossed, flat_s, velocity = refs[HALOS + 5 :]
    fill_extended(extended, own[...], *stacked_halos(halos, 0))

    def finish(x):
        value = face_mean(velocity, x)
        speed[x, :, :] = value
        out[x, :, :] = base[x, :, :] - push[x, :, :] * value

    speed_stages(extended, matrices, crossed, flat_s, velocity, finish)


def later_kernel(own, *refs):
    halos = refs[: HALOS + 1]
    matrices, gain, speed, out = refs[HALOS + 1 : HALOS + 5]
    extended, crossed, flat_s, flat_g, normals, lengths = refs[HALOS + 5 :]
    fill_extended(extended, own[...], *[halo[...] for halo in halos])

    def finish(x):
        factor = gain[x // (SIDE // 2), :, :] * lengths[x + 1, 0:SIDE, :]
        out[x, :, :] = own[x, :, :] - factor * (speed[x, :, :] - bending(normals, x))

    gradient_stages(extended, matrices, crossed, flat_s, flat_g, normals, lengths, finish)


def call_kernel(body, arrays, outputs, scratch):
    shape = jax.ShapeDtypeStruct((SIDE, SIDE, DEPTH), jnp.float32)
    return pl.pallas_call(
        body,
        out_shape=(shape,) * outputs,
        in_specs=[VMEM] * len(arrays),
        out_specs=(VMEM,) * outputs,
        scratch_shapes=[pltpu.VMEM(shape, jnp.float32) for shape in scratch],
        compiler_params=pltpu.CompilerParams(vmem_limit_bytes=20 * 1024 * 1024),
    )(*arrays)


def corner_kernel(own, x_even, x_odd, even, odd):
    parity = lax.axis_index("gy") & 1
    starts = [
        pl.multiple_of(jnp.where(parity == side, SIDE - SLAB, 0), SLAB) for side in range(2)
    ]
    offset = even.shape[0] - 2 * REACH
    if offset:
        even[0:SIDE, :, :] = own[:, pl.ds(starts[0], SLAB), :]
    for at, source in enumerate((x_even, x_odd)):
        rows = slice(at * REACH, (at + 1) * REACH)
        even[offset + rows.start : offset + rows.stop, :, :] = source[:, pl.ds(starts[0], SLAB), :]
        odd[rows, :, :] = source[:, pl.ds(starts[1], SLAB), :]


def corner_sides(own, x_halos, offset=0):
    return pl.pallas_call(
        corner_kernel,
        out_shape=(
            jax.ShapeDtypeStruct((offset + 2 * REACH, SLAB, DEPTH), jnp.float32),
            jax.ShapeDtypeStruct((2 * REACH, SLAB, DEPTH), jnp.float32),
        ),
        in_specs=[VMEM] * 3,
        out_specs=(VMEM, VMEM),
        compiler_params=SMALL,
    )(own, *x_halos)


def copy_kernel(source, target):
    target[...] = source[...]


def settle(block):
    return pl.pallas_call(
        copy_kernel,
        out_shape=jax.ShapeDtypeStruct(block.shape, block.dtype),
        in_specs=[VMEM],
        out_specs=VMEM,
        compiler_params=SMALL,
    )(block)


def swap(block, axis, first):
    pairs = []
    for low in range(first, lax.axis_size(axis) - 1, 2):
        pairs += [(low, low + 1), (low + 1, low)]
    return lax.ppermute(block, axis, pairs)


def both_sides(block, dim, width, parity):
    length = block.shape[dim]
    high = jnp.where(parity == 0, length - width, 0)
    return (
        lax.dynamic_slice_in_dim(block, high, width, dim),
        lax.dynamic_slice_in_dim(block, length - width - high, width, dim),
    )


def swap_sides(pieces, axis):
    odd = swap(pieces[1], axis, 1)
    even = swap(pieces[0], axis, 0)
    return even, odd


def per_device(level_set, sensitivity, smooth_taps, slope_taps, band, time_step):
    parity = [lax.axis_index(axis) & 1 for axis in ("gx", "gy")]
    fields = [sensitivity, level_set]
    x_halos = swap_sides(both_sides(level_set, 0, REACH, parity[0]), "gx")
    x_halos_s = swap_sides(both_sides(sensitivity, 0, REACH, parity[0]), "gx")
    y_odd = swap(jnp.stack([both_sides(f, 1, SLAB, parity[1])[1] for f in fields]), "gy", 1)
    matrices = prepare(smooth_taps, slope_taps, band, time_step)
    x_halos = (x_halos[0], settle(x_halos[1]))
    matrices, gain = matrices
    pieces = corner_sides(level_set, x_halos, SIDE)
    corners = swap_sides(pieces, "gy")
    x_odd, matrices, gain = lax.optimization_barrier((x_halos_s[1], matrices, gain))
    x_halos_s = (x_halos_s[0], settle(x_odd))
    corners_s = swap_sides(corner_sides(sensitivity, x_halos_s, SIDE), "gy")
    rim = SIDE + 2
    gradient_scratch = [
        (WIDE, WIDE + 8, DEPTH), (WIDE, 2 * RIM + 8, DEPTH), (rim, 2 * RIM, DEPTH),
        (rim, RIM, DEPTH), (3, rim, RIM, DEPTH), (rim, RIM, DEPTH),
    ]
    speed_scratch = [
        (WIDE, WIDE + 8, DEPTH), (WIDE, RIM + 16, DEPTH), (rim, RIM, DEPTH), (rim, RIM, DEPTH)
    ]
    base, push = call_kernel(
        bend_kernel, (level_set, *x_halos, y_odd, *corners, matrices, gain), 2, gradient_scratch
    )
    phi, speed = call_kernel(
        speed_kernel, (sensitivity, *x_halos_s, y_odd, *corners_s, matrices, base, push), 2,
        speed_scratch,
    )
    for _ in range(1, UPDATES):
        x_halos = swap_sides(both_sides(phi, 0, REACH, parity[0]), "gx")
        y_halos = swap_sides(both_sides(phi, 1, SLAB, parity[1]), "gy")
        x_halos = (x_halos[0], settle(x_halos[1]))
        corners = swap_sides(corner_sides(phi, x_halos), "gy")
        y_halos = (y_halos[0], settle(y_halos[1]))
        (phi,) = call_kernel(
            later_kernel, (phi, *x_halos, *y_halos, *corners, matrices, gain, speed), 1, gradient_scratch,
        )
    return phi


def solution(mesh):
    return jax.shard_map(
        per_device,
        mesh=mesh,
        in_specs=(P("gx", "gy", None), P("gx", "gy", None), P(), P(), P("gx", "gy", None), P()),
        out_specs=P("gx", "gy", None),
        check_vma=False,
    )
```

```python
import jax
import jax.numpy as jnp
from jax import lax
from jax.experimental import pallas as pl
from jax.experimental.pallas import tpu as pltpu
from jax.sharding import PartitionSpec as P

UPDATES = 2
REACH = 13
SLAB = 16
SIDE = 32
RIM = 40
WIDE = 64
DEPTH = 128
TAPS = 25

OUT_ROWS = [RIM - 1] + list(range(SIDE + 1))


def split_rows(value):
    high = value.astype(jnp.bfloat16)
    low = (value - high.astype(jnp.float32)).astype(jnp.bfloat16)
    return high, low


def tap_select(index, taps):
    total = jnp.zeros(index.shape, jnp.float32)
    for k in range(TAPS):
        total = jnp.where(index == k, taps[k], total)
    return total


def side_matrix(axis, smooth, slope):
    at = lax.axis_index(axis)
    last = lax.axis_size(axis) - 1
    shape = (RIM, 3 * WIDE)
    row = lax.broadcasted_iota(jnp.int32, shape, 0)
    column = lax.broadcasted_iota(jnp.int32, shape, 1)
    place = column & (WIDE - 1)
    width = REACH if axis == "gx" else SLAB
    source = place
    for slot, side in ((0, at & 1), (1, 1 - (at & 1))):
        start = SIDE + slot * SLAB
        moved = place - start + jnp.where(side == 0, SIDE, -width)
        source = jnp.where((place >= start) & (place < start + SLAB), moved, source)
        source = jnp.where((place >= start + width) & (place < start + SLAB), -WIDE, source)
    target = jnp.where(row < RIM - 1, row, -1)
    index = source - target + TAPS // 2
    inside = (row < SIDE) | ((row == SIDE) & (at < last)) | ((row == RIM - 1) & (at > 0))
    index = jnp.where(inside, index, -1)
    parts = []
    for taps in (smooth, slope):
        full = tap_select(index, taps)
        high = full.astype(jnp.bfloat16).astype(jnp.float32)
        parts.append(jnp.where(column < 2 * WIDE, high, full - high))
    return jnp.concatenate(parts, axis=0).astype(jnp.bfloat16)


def block_gain(band, step, p):
    blocks_y, blocks_z = 2, 4
    rows = SIDE // blocks_y
    lane = lax.broadcasted_iota(jnp.int32, (rows, DEPTH), 1) // (DEPTH // blocks_z)
    parts = []
    for q in range(blocks_y):
        value = jnp.zeros(lane.shape, jnp.float32)
        for r in range(blocks_z):
            entry = band[p, q, r].astype(jnp.float32) * step[0]
            value = jnp.where(lane == r, entry, value)
        parts.append(value)
    return jnp.concatenate(parts, axis=0)


def prepare_kernel(smooth, slope, band, step, out, gain):
    for p in range(2):
        gain[p, :, :] = block_gain(band, step, p)
    for at, axis in enumerate(("gx", "gy")):
        out[2 * at * RIM : 2 * (at + 1) * RIM, 0 : 3 * WIDE] = side_matrix(axis, smooth, slope)
        out[2 * at * RIM : 2 * (at + 1) * RIM, 3 * WIDE :] = jnp.zeros((2 * RIM, WIDE), jnp.bfloat16)
    shape = (DEPTH, DEPTH)
    index = (
        lax.broadcasted_iota(jnp.int32, shape, 0)
        - lax.broadcasted_iota(jnp.int32, shape, 1)
        + TAPS // 2
    )
    for at, taps in enumerate((smooth, slope)):
        columns = slice(at * DEPTH, (at + 1) * DEPTH)
        high, low = split_rows(tap_select(index, taps))
        out[4 * RIM : 4 * RIM + DEPTH, columns] = high
        out[4 * RIM + DEPTH : 4 * RIM + 2 * DEPTH, columns] = high
        out[4 * RIM + 2 * DEPTH :, columns] = low


SMEM = pl.BlockSpec(memory_space=pltpu.SMEM)
VMEM = pl.BlockSpec(memory_space=pltpu.VMEM)
SMALL = pltpu.CompilerParams(vmem_limit_bytes=4 * 1024 * 1024)


def prepare(smooth, slope, band, step):
    return pl.pallas_call(
        prepare_kernel,
        out_shape=(
            jax.ShapeDtypeStruct((4 * RIM + 3 * DEPTH, 2 * DEPTH), jnp.bfloat16),
            jax.ShapeDtypeStruct((2, SIDE, DEPTH), jnp.float32),
        ),
        in_specs=[SMEM] * 4,
        out_specs=(VMEM, VMEM),
        compiler_params=SMALL,
        cost_estimate=pl.CostEstimate(flops=1000000, bytes_accessed=1000000, transcendentals=0),
    )(smooth, slope, band, step)


def along_matrix(matrices, axis, rows):
    return matrices[2 * axis * RIM : 2 * axis * RIM + rows, 0 : 3 * WIDE]


def depth_matrix(matrices, kind):
    return matrices[4 * RIM :, kind * DEPTH : (kind + 1) * DEPTH]


def fill_extended(extended, own, x_even, x_odd, y_even, y_odd, even_corner, odd_corner):
    extended[0:SIDE, 0:SIDE, :] = own
    gap = jnp.zeros((SLAB - REACH, WIDE, DEPTH), jnp.float32)
    columns = (slice(SIDE, SIDE + SLAB), slice(SIDE + SLAB, WIDE))
    extended[0:SIDE, columns[0], :] = y_even
    extended[0:SIDE, columns[1], :] = y_odd
    for at, part in enumerate((x_even, x_odd)):
        rows = slice(SIDE + at * SLAB, SIDE + at * SLAB + REACH)
        extended[rows, 0:SIDE, :] = part
        extended[rows.stop : SIDE + (at + 1) * SLAB, 0:WIDE, :] = gap
        extended[rows, columns[0], :] = even_corner[at * REACH : (at + 1) * REACH]
        extended[rows, columns[1], :] = odd_corner[at * REACH : (at + 1) * REACH]


def stacked_parts(value):
    high, low = split_rows(value)
    return jnp.concatenate([high, low, high], axis=0)


def lane_parts(value):
    high, low = split_rows(value)
    return jnp.concatenate([high, low, high], axis=1)


def take_place(block, place):
    outer, inner, depth = block.shape
    return block.reshape(outer * inner, depth)[pl.ds(place, outer, stride=inner), :]


def along_x_stage(extended, crossed, matrix):
    for pair in range(0, WIDE, 2):
        places = (pair, pair + 1)
        value = jnp.concatenate([take_place(extended, y) for y in places], axis=1)
        out = jnp.dot(matrix, stacked_parts(value), preferred_element_type=jnp.float32)
        for at, y in enumerate(places):
            crossed[y, 0 : out.shape[0], :] = out[:, at * DEPTH : (at + 1) * DEPTH]


def gradient_stages(extended, matrices, crossed, flat_s, flat_g, normals, lengths, finish):
    along_x_stage(extended, crossed, along_matrix(matrices, 0, 2 * RIM))
    matrix = along_matrix(matrices, 1, 2 * RIM)
    for at, row in enumerate(OUT_ROWS):
        value = jnp.concatenate(
            [take_place(crossed, row + kind * RIM) for kind in range(2)], axis=1
        )
        got = jnp.dot(matrix, stacked_parts(value), preferred_element_type=jnp.float32)
        flat_s[at, 0:RIM, :] = got[0:RIM, DEPTH:]
        flat_s[at, RIM:, :] = got[RIM:, :DEPTH]
        flat_g[at, :, :] = got[0:RIM, :DEPTH]
    weights_s = depth_matrix(matrices, 0)
    weights_g = depth_matrix(matrices, 1)
    for at in range(0, SIDE + 2, 2):
        cross = jnp.dot(
            lane_parts(flat_s[at : at + 2].reshape(4 * RIM, DEPTH)), weights_s,
            preferred_element_type=jnp.float32,
        )
        deep = jnp.dot(
            lane_parts(flat_g[at : at + 2].reshape(2 * RIM, DEPTH)), weights_g,
            preferred_element_type=jnp.float32,
        )
        for half in range(2):
            grad_x = cross[2 * half * RIM : (2 * half + 1) * RIM]
            grad_y = cross[(2 * half + 1) * RIM : (2 * half + 2) * RIM]
            grad_z = deep[half * RIM : (half + 1) * RIM]
            square = grad_x * grad_x + grad_y * grad_y + grad_z * grad_z + 1.0
            inverse = lax.rsqrt(square)
            normals[0, at + half, :, :] = grad_x * inverse
            normals[1, at + half, :, :] = grad_y * inverse
            normals[2, at + half, :, :] = grad_z * inverse
            lengths[at + half, :, :] = square * inverse
        if at > 0:
            finish(at - 2)
            finish(at - 1)


def bending(normals, x):
    lane = lax.broadcasted_iota(jnp.int32, (SIDE, DEPTH), 1)
    at = x + 1
    across = normals[1, at, :, :]
    deep = normals[2, at, 0:SIDE, :]
    bend = normals[0, at + 1, 0:SIDE, :] - normals[0, at - 1, 0:SIDE, :]
    bend += (pltpu.roll(across, RIM - 1, 0) - pltpu.roll(across, 1, 0))[0:SIDE]
    bend += jnp.where(lane < DEPTH - 1, pltpu.roll(deep, DEPTH - 1, 1), 0.0)
    bend -= jnp.where(lane > 0, pltpu.roll(deep, 1, 1), 0.0)
    return 0.25 * bend


def speed_stages(extended, matrices, crossed, flat_s, velocity, finish):
    along_x_stage(extended, crossed, along_matrix(matrices, 0, RIM + 8))
    matrix = along_matrix(matrices, 1, RIM + 8)
    for pair in range(0, len(OUT_ROWS), 2):
        value = jnp.concatenate(
            [take_place(crossed, row) for row in OUT_ROWS[pair : pair + 2]], axis=1
        )
        got = jnp.dot(matrix, stacked_parts(value), preferred_element_type=jnp.float32)
        for half in range(2):
            flat_s[pair + half, :, :] = got[0:RIM, half * DEPTH : (half + 1) * DEPTH]
    weights = depth_matrix(matrices, 0)
    for at in range(0, SIDE + 2, 2):
        got = jnp.dot(
            lane_parts(flat_s[at : at + 2].reshape(2 * RIM, DEPTH)), weights,
            preferred_element_type=jnp.float32,
        )
        velocity[at : at + 2, :, :] = got.reshape(2, RIM, DEPTH)
        if at > 0:
            finish(at - 2)
            finish(at - 1)


def face_mean(velocity, x):
    lane = lax.broadcasted_iota(jnp.int32, (SIDE, DEPTH), 1)
    at = x + 1
    rim = velocity[at, :, :]
    centre = rim[0:SIDE]
    total = centre + velocity[at + 1, 0:SIDE, :] + velocity[at - 1, 0:SIDE, :]
    total += (pltpu.roll(rim, RIM - 1, 0) + pltpu.roll(rim, 1, 0))[0:SIDE]
    total += jnp.where(lane < DEPTH - 1, pltpu.roll(centre, DEPTH - 1, 1), 0.0)
    total += jnp.where(lane > 0, pltpu.roll(centre, 1, 1), 0.0)
    return total * (1.0 / 7.0)


HALOS = 5


def stacked_halos(halos, part):
    x_even, x_odd, even_slab, odd_corner = [halos[at][...] for at in (0, 1, 3, 4)]
    return x_even, x_odd, even_slab[0:SIDE], halos[2][part], even_slab[SIDE:], odd_corner


def bend_kernel(own, *refs):
    halos = refs[:HALOS]
    matrices, gain, base, push = refs[HALOS : HALOS + 4]
    extended, crossed, flat_s, flat_g, normals, lengths = refs[HALOS + 4 :]
    fill_extended(extended, own[...], *stacked_halos(halos, 1))

    def finish(x):
        factor = gain[x // (SIDE // 2), :, :] * lengths[x + 1, 0:SIDE, :]
        push[x, :, :] = factor
        base[x, :, :] = own[x, :, :] + factor * bending(normals, x)

    gradient_stages(extended, matrices, crossed, flat_s, flat_g, normals, lengths, finish)


def speed_kernel(own, *refs):
    halos = refs[:HALOS]
    matrices, base, push, out, speed = refs[HALOS : HALOS + 5]
    extended, crossed, flat_s, velocity = refs[HALOS + 5 :]
    fill_extended(extended, own[...], *stacked_halos(halos, 0))

    def finish(x):
        value = face_mean(velocity, x)
        speed[x, :, :] = value
        out[x, :, :] = base[x, :, :] - push[x, :, :] * value

    speed_stages(extended, matrices, crossed, flat_s, velocity, finish)


CHUNK = 8


def later_kernel(own, *refs):
    halos = refs[: HALOS + 1]
    matrices, gain, speed, out = refs[HALOS + 1 : HALOS + 5]
    extended, crossed, flat_s, flat_g, normals, lengths, result, sems = refs[HALOS + 5 :]
    fill_extended(extended, own[...], *[halo[...] for halo in halos])

    copies = [
        pltpu.make_async_copy(
            result.at[pl.ds(at * CHUNK, CHUNK)], out.at[pl.ds(at * CHUNK, CHUNK)], sems.at[at]
        )
        for at in range(SIDE // CHUNK)
    ]

    def finish(x):
        factor = gain[x // (SIDE // 2), :, :] * lengths[x + 1, 0:SIDE, :]
        result[x, :, :] = own[x, :, :] - factor * (speed[x, :, :] - bending(normals, x))
        if x % CHUNK == CHUNK - 1:
            copies[x // CHUNK].start()

    gradient_stages(extended, matrices, crossed, flat_s, flat_g, normals, lengths, finish)
    for copy in copies:
        copy.wait()


def call_kernel(body, arrays, outputs, scratch, out_spec=VMEM, extra=()):
    shape = jax.ShapeDtypeStruct((SIDE, SIDE, DEPTH), jnp.float32)
    return pl.pallas_call(
        body,
        out_shape=(shape,) * outputs,
        in_specs=[VMEM] * len(arrays),
        out_specs=(out_spec,) * outputs,
        scratch_shapes=[pltpu.VMEM(shape, jnp.float32) for shape in scratch] + list(extra),
        compiler_params=pltpu.CompilerParams(vmem_limit_bytes=20 * 1024 * 1024),
    )(*arrays)


def corner_kernel(own, x_even, x_odd, even, odd):
    parity = lax.axis_index("gy") & 1
    starts = [
        pl.multiple_of(jnp.where(parity == side, SIDE - SLAB, 0), SLAB) for side in range(2)
    ]
    offset = even.shape[0] - 2 * REACH
    if offset:
        even[0:SIDE, :, :] = own[:, pl.ds(starts[0], SLAB), :]
    for at, source in enumerate((x_even, x_odd)):
        rows = slice(at * REACH, (at + 1) * REACH)
        even[offset + rows.start : offset + rows.stop, :, :] = source[:, pl.ds(starts[0], SLAB), :]
        odd[rows, :, :] = source[:, pl.ds(starts[1], SLAB), :]


def corner_sides(own, x_halos, offset=0):
    return pl.pallas_call(
        corner_kernel,
        out_shape=(
            jax.ShapeDtypeStruct((offset + 2 * REACH, SLAB, DEPTH), jnp.float32),
            jax.ShapeDtypeStruct((2 * REACH, SLAB, DEPTH), jnp.float32),
        ),
        in_specs=[VMEM] * 3,
        out_specs=(VMEM, VMEM),
        compiler_params=SMALL,
    )(own, *x_halos)


def copy_kernel(source, target):
    target[...] = source[...]


def settle(block):
    return pl.pallas_call(
        copy_kernel,
        out_shape=jax.ShapeDtypeStruct(block.shape, block.dtype),
        in_specs=[VMEM],
        out_specs=VMEM,
        compiler_params=SMALL,
    )(block)


def swap(block, axis, first):
    pairs = []
    for low in range(first, lax.axis_size(axis) - 1, 2):
        pairs += [(low, low + 1), (low + 1, low)]
    return lax.ppermute(block, axis, pairs)


def both_sides(block, dim, width, parity):
    length = block.shape[dim]
    high = jnp.where(parity == 0, length - width, 0)
    return (
        lax.dynamic_slice_in_dim(block, high, width, dim),
        lax.dynamic_slice_in_dim(block, length - width - high, width, dim),
    )


def swap_sides(pieces, axis):
    odd = swap(pieces[1], axis, 1)
    even = swap(pieces[0], axis, 0)
    return even, odd


def per_device(level_set, sensitivity, smooth_taps, slope_taps, band, time_step):
    parity = [lax.axis_index(axis) & 1 for axis in ("gx", "gy")]
    fields = [sensitivity, level_set]
    x_halos = swap_sides(both_sides(level_set, 0, REACH, parity[0]), "gx")
    x_halos_s = swap_sides(both_sides(sensitivity, 0, REACH, parity[0]), "gx")
    y_odd = swap(jnp.stack([both_sides(f, 1, SLAB, parity[1])[1] for f in fields]), "gy", 1)
    matrices = prepare(smooth_taps, slope_taps, band, time_step)
    x_halos = (x_halos[0], settle(x_halos[1]))
    matrices, gain = matrices
    pieces = corner_sides(level_set, x_halos, SIDE)
    corners = swap_sides(pieces, "gy")
    x_odd, matrices, gain = lax.optimization_barrier((x_halos_s[1], matrices, gain))
    x_halos_s = (x_halos_s[0], settle(x_odd))
    corners_s = swap_sides(corner_sides(sensitivity, x_halos_s, SIDE), "gy")
    rim = SIDE + 2
    gradient_scratch = [
        (WIDE, WIDE + 8, DEPTH), (WIDE, 2 * RIM + 8, DEPTH), (rim, 2 * RIM, DEPTH),
        (rim, RIM, DEPTH), (3, rim, RIM, DEPTH), (rim, RIM, DEPTH),
    ]
    speed_scratch = [
        (WIDE, WIDE + 8, DEPTH), (WIDE, RIM + 16, DEPTH), (rim, RIM, DEPTH), (rim, RIM, DEPTH)
    ]
    base, push = call_kernel(
        bend_kernel, (level_set, *x_halos, y_odd, *corners, matrices, gain), 2, gradient_scratch
    )
    phi, speed = call_kernel(
        speed_kernel, (sensitivity, *x_halos_s, y_odd, *corners_s, matrices, base, push), 2,
        speed_scratch,
    )
    for _ in range(1, UPDATES):
        x_halos = swap_sides(both_sides(phi, 0, REACH, parity[0]), "gx")
        y_halos = swap_sides(both_sides(phi, 1, SLAB, parity[1]), "gy")
        x_halos = (x_halos[0], settle(x_halos[1]))
        corners = swap_sides(corner_sides(phi, x_halos), "gy")
        y_halos = (y_halos[0], settle(y_halos[1]))
        (phi,) = call_kernel(
            later_kernel, (phi, *x_halos, *y_halos, *corners, matrices, gain, speed), 1, gradient_scratch + [(SIDE, SIDE, DEPTH)],
            pl.BlockSpec(memory_space=pl.ANY), (pltpu.SemaphoreType.DMA((SIDE // CHUNK,)),),
        )
    return phi


def solution(mesh):
    return jax.shard_map(
        per_device,
        mesh=mesh,
        in_specs=(P("gx", "gy", None), P("gx", "gy", None), P(), P(), P("gx", "gy", None), P()),
        out_specs=P("gx", "gy", None),
        check_vma=False,
    )
```

```python
import jax
import jax.numpy as jnp
from jax import lax
from jax.experimental import pallas as pl
from jax.experimental.pallas import tpu as pltpu
from jax.sharding import PartitionSpec as P

UPDATES = 2
REACH = 13
SLAB = 16
SIDE = 32
RIM = 40
WIDE = 64
DEPTH = 128
TAPS = 25

OUT_ROWS = [RIM - 1] + list(range(SIDE + 1))


def split_rows(value):
    high = value.astype(jnp.bfloat16)
    low = (value - high.astype(jnp.float32)).astype(jnp.bfloat16)
    return high, low


def tap_select(index, taps):
    total = jnp.zeros(index.shape, jnp.float32)
    for k in range(TAPS):
        total = jnp.where(index == k, taps[k], total)
    return total


def side_matrix(axis, smooth, slope):
    at = lax.axis_index(axis)
    last = lax.axis_size(axis) - 1
    shape = (RIM, 3 * WIDE)
    row = lax.broadcasted_iota(jnp.int32, shape, 0)
    column = lax.broadcasted_iota(jnp.int32, shape, 1)
    place = column & (WIDE - 1)
    width = REACH if axis == "gx" else SLAB
    source = place
    for slot, side in ((0, at & 1), (1, 1 - (at & 1))):
        start = SIDE + slot * SLAB
        moved = place - start + jnp.where(side == 0, SIDE, -width)
        source = jnp.where((place >= start) & (place < start + SLAB), moved, source)
        source = jnp.where((place >= start + width) & (place < start + SLAB), -WIDE, source)
    target = jnp.where(row < RIM - 1, row, -1)
    index = source - target + TAPS // 2
    inside = (row < SIDE) | ((row == SIDE) & (at < last)) | ((row == RIM - 1) & (at > 0))
    index = jnp.where(inside, index, -1)
    parts = []
    for taps in (smooth, slope):
        full = tap_select(index, taps)
        high = full.astype(jnp.bfloat16).astype(jnp.float32)
        parts.append(jnp.where(column < 2 * WIDE, high, full - high))
    return jnp.concatenate(parts, axis=0).astype(jnp.bfloat16)


def block_gain(band, step, p):
    blocks_y, blocks_z = 2, 4
    rows = SIDE // blocks_y
    lane = lax.broadcasted_iota(jnp.int32, (rows, DEPTH), 1) // (DEPTH // blocks_z)
    parts = []
    for q in range(blocks_y):
        value = jnp.zeros(lane.shape, jnp.float32)
        for r in range(blocks_z):
            entry = band[p, q, r].astype(jnp.float32) * step[0]
            value = jnp.where(lane == r, entry, value)
        parts.append(value)
    return jnp.concatenate(parts, axis=0)


def prepare_kernel(smooth, slope, band, step, out, gain):
    for p in range(2):
        gain[p, :, :] = block_gain(band, step, p)
    for at, axis in enumerate(("gx", "gy")):
        out[2 * at * RIM : 2 * (at + 1) * RIM, 0 : 3 * WIDE] = side_matrix(axis, smooth, slope)
        out[2 * at * RIM : 2 * (at + 1) * RIM, 3 * WIDE :] = jnp.zeros((2 * RIM, WIDE), jnp.bfloat16)
    shape = (DEPTH, DEPTH)
    index = (
        lax.broadcasted_iota(jnp.int32, shape, 0)
        - lax.broadcasted_iota(jnp.int32, shape, 1)
        + TAPS // 2
    )
    for at, taps in enumerate((smooth, slope)):
        columns = slice(at * DEPTH, (at + 1) * DEPTH)
        high, low = split_rows(tap_select(index, taps))
        out[4 * RIM : 4 * RIM + DEPTH, columns] = high
        out[4 * RIM + DEPTH : 4 * RIM + 2 * DEPTH, columns] = high
        out[4 * RIM + 2 * DEPTH :, columns] = low


SMEM = pl.BlockSpec(memory_space=pltpu.SMEM)
VMEM = pl.BlockSpec(memory_space=pltpu.VMEM)
SMALL = pltpu.CompilerParams(vmem_limit_bytes=4 * 1024 * 1024)


def prepare(smooth, slope, band, step):
    return pl.pallas_call(
        prepare_kernel,
        out_shape=(
            jax.ShapeDtypeStruct((4 * RIM + 3 * DEPTH, 2 * DEPTH), jnp.bfloat16),
            jax.ShapeDtypeStruct((2, SIDE, DEPTH), jnp.float32),
        ),
        in_specs=[SMEM] * 4,
        out_specs=(VMEM, VMEM),
        compiler_params=SMALL,
        cost_estimate=pl.CostEstimate(flops=1000000, bytes_accessed=1000000, transcendentals=0),
    )(smooth, slope, band, step)


def along_matrix(matrices, axis, rows):
    return matrices[2 * axis * RIM : 2 * axis * RIM + rows, 0 : 3 * WIDE]


def depth_matrix(matrices, kind):
    return matrices[4 * RIM :, kind * DEPTH : (kind + 1) * DEPTH]


def fill_extended(extended, own, x_even, x_odd, y_even, y_odd, even_corner, odd_corner):
    extended[0:SIDE, 0:SIDE, :] = own
    gap = jnp.zeros((SLAB - REACH, WIDE, DEPTH), jnp.float32)
    columns = (slice(SIDE, SIDE + SLAB), slice(SIDE + SLAB, WIDE))
    extended[0:SIDE, columns[0], :] = y_even
    extended[0:SIDE, columns[1], :] = y_odd
    for at, part in enumerate((x_even, x_odd)):
        rows = slice(SIDE + at * SLAB, SIDE + at * SLAB + REACH)
        extended[rows, 0:SIDE, :] = part
        extended[rows.stop : SIDE + (at + 1) * SLAB, 0:WIDE, :] = gap
        extended[rows, columns[0], :] = even_corner[at * REACH : (at + 1) * REACH]
        extended[rows, columns[1], :] = odd_corner[at * REACH : (at + 1) * REACH]


def stacked_parts(value):
    high, low = split_rows(value)
    return jnp.concatenate([high, low, high], axis=0)


def lane_parts(value):
    high, low = split_rows(value)
    return jnp.concatenate([high, low, high], axis=1)


def take_place(block, place):
    outer, inner, depth = block.shape
    return block.reshape(outer * inner, depth)[pl.ds(place, outer, stride=inner), :]


def along_x_stage(extended, crossed, matrix):
    for pair in range(0, WIDE, 2):
        places = (pair, pair + 1)
        value = jnp.concatenate([take_place(extended, y) for y in places], axis=1)
        out = jnp.dot(matrix, stacked_parts(value), preferred_element_type=jnp.float32)
        for at, y in enumerate(places):
            crossed[y, 0 : out.shape[0], :] = out[:, at * DEPTH : (at + 1) * DEPTH]


def gradient_stages(extended, matrices, crossed, flat_s, flat_g, normals, lengths, finish):
    along_x_stage(extended, crossed, along_matrix(matrices, 0, 2 * RIM))
    matrix = along_matrix(matrices, 1, 2 * RIM)
    for at, row in enumerate(OUT_ROWS):
        value = jnp.concatenate(
            [take_place(crossed, row + kind * RIM) for kind in range(2)], axis=1
        )
        got = jnp.dot(matrix, stacked_parts(value), preferred_element_type=jnp.float32)
        flat_s[at, 0:RIM, :] = got[0:RIM, DEPTH:]
        flat_s[at, RIM:, :] = got[RIM:, :DEPTH]
        flat_g[at, :, :] = got[0:RIM, :DEPTH]
    weights_s = depth_matrix(matrices, 0)
    weights_g = depth_matrix(matrices, 1)
    for at in range(0, SIDE + 2, 2):
        cross = jnp.dot(
            lane_parts(flat_s[at : at + 2].reshape(4 * RIM, DEPTH)), weights_s,
            preferred_element_type=jnp.float32,
        )
        deep = jnp.dot(
            lane_parts(flat_g[at : at + 2].reshape(2 * RIM, DEPTH)), weights_g,
            preferred_element_type=jnp.float32,
        )
        for half in range(2):
            grad_x = cross[2 * half * RIM : (2 * half + 1) * RIM]
            grad_y = cross[(2 * half + 1) * RIM : (2 * half + 2) * RIM]
            grad_z = deep[half * RIM : (half + 1) * RIM]
            square = grad_x * grad_x + grad_y * grad_y + grad_z * grad_z + 1.0
            inverse = lax.rsqrt(square)
            normals[0, at + half, :, :] = grad_x * inverse
            normals[1, at + half, :, :] = grad_y * inverse
            normals[2, at + half, :, :] = grad_z * inverse
            lengths[at + half, :, :] = square * inverse
        if at > 0:
            finish(at - 2)
            finish(at - 1)


def bending(normals, x):
    lane = lax.broadcasted_iota(jnp.int32, (SIDE, DEPTH), 1)
    at = x + 1
    across = normals[1, at, :, :]
    deep = normals[2, at, 0:SIDE, :]
    bend = normals[0, at + 1, 0:SIDE, :] - normals[0, at - 1, 0:SIDE, :]
    bend += (pltpu.roll(across, RIM - 1, 0) - pltpu.roll(across, 1, 0))[0:SIDE]
    bend += jnp.where(lane < DEPTH - 1, pltpu.roll(deep, DEPTH - 1, 1), 0.0)
    bend -= jnp.where(lane > 0, pltpu.roll(deep, 1, 1), 0.0)
    return 0.25 * bend


def speed_stages(extended, matrices, crossed, flat_s, velocity, finish):
    along_x_stage(extended, crossed, along_matrix(matrices, 0, RIM + 8))
    matrix = along_matrix(matrices, 1, RIM + 8)
    for pair in range(0, len(OUT_ROWS), 2):
        value = jnp.concatenate(
            [take_place(crossed, row) for row in OUT_ROWS[pair : pair + 2]], axis=1
        )
        got = jnp.dot(matrix, stacked_parts(value), preferred_element_type=jnp.float32)
        for half in range(2):
            flat_s[pair + half, :, :] = got[0:RIM, half * DEPTH : (half + 1) * DEPTH]
    weights = depth_matrix(matrices, 0)
    for at in range(0, SIDE + 2, 2):
        got = jnp.dot(
            lane_parts(flat_s[at : at + 2].reshape(2 * RIM, DEPTH)), weights,
            preferred_element_type=jnp.float32,
        )
        velocity[at : at + 2, :, :] = got.reshape(2, RIM, DEPTH)
        if at > 0:
            finish(at - 2)
            finish(at - 1)


def face_mean(velocity, x):
    lane = lax.broadcasted_iota(jnp.int32, (SIDE, DEPTH), 1)
    at = x + 1
    rim = velocity[at, :, :]
    centre = rim[0:SIDE]
    total = centre + velocity[at + 1, 0:SIDE, :] + velocity[at - 1, 0:SIDE, :]
    total += (pltpu.roll(rim, RIM - 1, 0) + pltpu.roll(rim, 1, 0))[0:SIDE]
    total += jnp.where(lane < DEPTH - 1, pltpu.roll(centre, DEPTH - 1, 1), 0.0)
    total += jnp.where(lane > 0, pltpu.roll(centre, 1, 1), 0.0)
    return total * (1.0 / 7.0)


HALOS = 5


def stacked_halos(halos, part):
    x_even, x_odd, even_slab, odd_corner = [halos[at][...] for at in (0, 1, 3, 4)]
    return x_even, x_odd, even_slab[0:SIDE], halos[2][part], even_slab[SIDE:], odd_corner


def bend_kernel(own, *refs):
    halos = refs[:HALOS]
    matrices, gain, base, push = refs[HALOS : HALOS + 4]
    extended, crossed, flat_s, flat_g, normals, lengths = refs[HALOS + 4 :]
    fill_extended(extended, own[...], *stacked_halos(halos, 1))

    def finish(x):
        factor = gain[x // (SIDE // 2), :, :] * lengths[x + 1, 0:SIDE, :]
        push[x, :, :] = factor
        base[x, :, :] = own[x, :, :] + factor * bending(normals, x)

    gradient_stages(extended, matrices, crossed, flat_s, flat_g, normals, lengths, finish)


def speed_kernel(own, *refs):
    halos = refs[:HALOS]
    matrices, base, push, out, speed = refs[HALOS : HALOS + 5]
    extended, crossed, flat_s, velocity = refs[HALOS + 5 :]
    fill_extended(extended, own[...], *stacked_halos(halos, 0))

    def finish(x):
        value = face_mean(velocity, x)
        speed[x, :, :] = value
        out[x, :, :] = base[x, :, :] - push[x, :, :] * value

    speed_stages(extended, matrices, crossed, flat_s, velocity, finish)


def later_kernel(own, *refs):
    halos = refs[: HALOS + 1]
    matrices, gain, speed, out = refs[HALOS + 1 : HALOS + 5]
    extended, crossed, flat_s, flat_g, normals, lengths = refs[HALOS + 5 :]
    fill_extended(extended, own[...], *[halo[...] for halo in halos])

    def finish(x):
        factor = gain[x // (SIDE // 2), :, :] * lengths[x + 1, 0:SIDE, :]
        out[x, :, :] = own[x, :, :] - factor * (speed[x, :, :] - bending(normals, x))

    gradient_stages(extended, matrices, crossed, flat_s, flat_g, normals, lengths, finish)


def call_kernel(body, arrays, outputs, scratch):
    shape = jax.ShapeDtypeStruct((SIDE, SIDE, DEPTH), jnp.float32)
    return pl.pallas_call(
        body,
        out_shape=(shape,) * outputs,
        in_specs=[VMEM] * len(arrays),
        out_specs=(VMEM,) * outputs,
        scratch_shapes=[pltpu.VMEM(shape, jnp.float32) for shape in scratch],
        compiler_params=pltpu.CompilerParams(vmem_limit_bytes=20 * 1024 * 1024),
    )(*arrays)


def corner_kernel(own, x_even, x_odd, even, odd):
    parity = lax.axis_index("gy") & 1
    starts = [
        pl.multiple_of(jnp.where(parity == side, SIDE - SLAB, 0), SLAB) for side in range(2)
    ]
    offset = even.shape[0] - 2 * REACH
    if offset:
        even[0:SIDE, :, :] = own[:, pl.ds(starts[0], SLAB), :]
    for at, source in enumerate((x_even, x_odd)):
        rows = slice(at * REACH, (at + 1) * REACH)
        even[offset + rows.start : offset + rows.stop, :, :] = source[:, pl.ds(starts[0], SLAB), :]
        odd[rows, :, :] = source[:, pl.ds(starts[1], SLAB), :]


def corner_sides(own, x_halos, offset=0):
    return pl.pallas_call(
        corner_kernel,
        out_shape=(
            jax.ShapeDtypeStruct((offset + 2 * REACH, SLAB, DEPTH), jnp.float32),
            jax.ShapeDtypeStruct((2 * REACH, SLAB, DEPTH), jnp.float32),
        ),
        in_specs=[VMEM] * 3,
        out_specs=(VMEM, VMEM),
        compiler_params=SMALL,
    )(own, *x_halos)


def copy_kernel(source, target):
    target[...] = source[...]


def settle(block):
    return pl.pallas_call(
        copy_kernel,
        out_shape=jax.ShapeDtypeStruct(block.shape, block.dtype),
        in_specs=[VMEM],
        out_specs=VMEM,
        compiler_params=SMALL,
    )(block)


def swap(block, axis, first):
    pairs = []
    for low in range(first, lax.axis_size(axis) - 1, 2):
        pairs += [(low, low + 1), (low + 1, low)]
    return lax.ppermute(block, axis, pairs)


def both_sides(block, dim, width, parity):
    length = block.shape[dim]
    high = jnp.where(parity == 0, length - width, 0)
    return (
        lax.dynamic_slice_in_dim(block, high, width, dim),
        lax.dynamic_slice_in_dim(block, length - width - high, width, dim),
    )


def swap_sides(pieces, axis):
    odd = swap(pieces[1], axis, 1)
    even = swap(pieces[0], axis, 0)
    return even, odd


def per_device(level_set, sensitivity, smooth_taps, slope_taps, band, time_step):
    parity = [lax.axis_index(axis) & 1 for axis in ("gx", "gy")]
    fields = [sensitivity, level_set]
    x_halos = swap_sides(both_sides(level_set, 0, REACH, parity[0]), "gx")
    x_halos_s = swap_sides(both_sides(sensitivity, 0, REACH, parity[0]), "gx")
    y_odd = swap(jnp.stack([both_sides(f, 1, SLAB, parity[1])[1] for f in fields]), "gy", 1)
    matrices = prepare(smooth_taps, slope_taps, band, time_step)
    x_halos = (x_halos[0], settle(x_halos[1]))
    matrices, gain = matrices
    pieces = corner_sides(level_set, x_halos, SIDE)
    corners = swap_sides(pieces, "gy")
    x_odd, matrices, gain = lax.optimization_barrier((x_halos_s[1], matrices, gain))
    x_halos_s = (x_halos_s[0], settle(x_odd))
    corners_s = swap_sides(corner_sides(sensitivity, x_halos_s, SIDE), "gy")
    rim = SIDE + 2
    gradient_scratch = [
        (WIDE, WIDE + 8, DEPTH), (WIDE, 2 * RIM + 8, DEPTH), (rim, 2 * RIM, DEPTH),
        (rim, RIM, DEPTH), (3, rim, RIM, DEPTH), (rim, RIM, DEPTH),
    ]
    speed_scratch = [
        (WIDE, WIDE + 8, DEPTH), (WIDE, RIM + 16, DEPTH), (rim, RIM, DEPTH), (rim, RIM, DEPTH)
    ]
    base, push = call_kernel(
        bend_kernel, (level_set, *x_halos, y_odd, *corners, matrices, gain), 2, gradient_scratch
    )
    phi, speed = call_kernel(
        speed_kernel, (sensitivity, *x_halos_s, y_odd, *corners_s, matrices, base, push), 2,
        speed_scratch,
    )
    for _ in range(1, UPDATES):
        x_halos = swap_sides(both_sides(phi, 0, REACH, parity[0]), "gx")
        y_halos = swap_sides(both_sides(phi, 1, SLAB, parity[1]), "gy")
        x_halos = (x_halos[0], settle(x_halos[1]))
        corners = swap_sides(corner_sides(phi, x_halos), "gy")
        (phi,) = call_kernel(
            later_kernel, (phi, *x_halos, *y_halos, *corners, matrices, gain, speed), 1, gradient_scratch,
        )
    return phi


def solution(mesh):
    return jax.shard_map(
        per_device,
        mesh=mesh,
        in_specs=(P("gx", "gy", None), P("gx", "gy", None), P(), P(), P("gx", "gy", None), P()),
        out_specs=P("gx", "gy", None),
        check_vma=False,
    )
```
